256 devices in a mesh: pb: 2 (over core), pas: 16 (over x, z_lo), tp: 8 (over z_hi, y).
Axes of the slice: x: 4, y: 4, z: 8 (z_hi: 2, z_lo: 4; z = z_hi * 4 + z_lo), core: 2. Of those that a mesh axis runs over, the one named last changes fastest.
Arguments:
- token_ids: int32 [8], P('pb'), parts along dimension 0, may hold values from 0 to 32127
- embedding: bfloat16 [32128, 4096], P(('pas', 'tp')), may hold values from -6 to 6
- passages: bfloat16 [16384, 4096], P(('pb', 'pas'), 'tp'), parts along dimension 0, may hold values from -6 to 6
- passage_lengths: int32 [64], P(('pb', 'pas')), parts along dimension 0, may hold values from 32 to 256
- w_key: bfloat16 [4096, 4096], P('pas', 'tp'), may hold values from -0.09375 to 0.09375
- w_value: bfloat16 [4096, 4096], P('pas', 'tp'), may hold values from -0.09375 to 0.09375
- norm_self: float32 [4096], replicated, may hold values from 0.1 to 1.9
- w_self_query: bfloat16 [4096, 4096], P('pas', 'tp'), may hold values from -1 to 1
- w_self_key: bfloat16 [4096, 4096], P('pas', 'tp'), may hold values from -0.09375 to 0.09375
- w_self_value: bfloat16 [4096, 4096], P('pas', 'tp'), may hold values from -0.09375 to 0.09375
- w_self_out: bfloat16 [4096, 4096], P('tp', 'pas'), may hold values from -0.09375 to 0.09375
- norm_cross: float32 [4096], replicated, may hold values from 0.1 to 1.9
- w_cross_query: bfloat16 [4096, 4096], P('pas', 'tp'), may hold values from -1 to 1
- w_cross_out: bfloat16 [4096, 4096], P('tp', 'pas'), may hold values from -0.09375 to 0.09375
- norm_ffn: float32 [4096], replicated, may hold values from 0.1 to 1.9
- w_gate: bfloat16 [4096, 10240], P('pas', 'tp'), may hold values from -0.09375 to 0.09375
- w_up: bfloat16 [4096, 10240], P('pas', 'tp'), may hold values from -0.09375 to 0.09375
- w_down: bfloat16 [10240, 4096], P('tp', 'pas'), may hold values from -0.0625 to 0.0625
Outputs:
- layer_out: float32 [8, 4096], P('pb', ('pas', 'tp')), parts along dimension 0
- cross_keys: bfloat16 [16384, 4096], P(('pb', 'pas'), 'tp'), parts along dimension 0
- cross_values: bfloat16 [16384, 4096], P(('pb', 'pas'), 'tp'), parts along dimension 0
The draws below stay inside these ranges and needn't reach their ends.
There are 2 independent parts, one for each index of `pb`. The reference program is written for one: setup_inputs(seed, part) draws one part's arguments, and reference() takes and returns one part's arrays. A program takes and returns all parts, laid end to end along the dimension named above; an argument that names none is the same for every part. Nothing has to cross between parts.
All inputs are finite; a program needn't handle non-finite values.
Results may differ from the reference program's by a relative error of at most 0.025.
Values may be sent and summed in bfloat16 or wider, within the bound.
A program may use at most 128 MiB of HBM per device.

```python
import math
import jax
import jax.numpy as jnp
import numpy as np
from jax import lax

D = 4096
H = 64
DH = 64
FF = 10240
VOCAB = 32128
PLEN = 256
STEPS = 4
PASS = 32
NTOK = 8192


def head_factors(key, heads, top, lowest):
    position = jax.random.permutation(key, heads)
    strong = heads // 4
    span = jnp.log(top / lowest)
    factor = top * jnp.exp(-span * position.astype(jnp.float32) / float(max(strong - 1, 1)))
    return jnp.where(position < strong, factor, 1.0)


def shaped_query(base, key, top, lowest):
    factor = head_factors(key, H, top, lowest)
    columns = jnp.repeat(factor, DH)
    return (base * columns[None, :] / float(DH)).astype(jnp.bfloat16)


def draw_w_self_query(key, part):
    key = jax.random.fold_in(key, 11)
    key_rank, key_base = jax.random.split(key)
    base = jnp.clip(jax.random.normal(key_base, (D, H * DH), jnp.float32), -4.0, 4.0)
    return shaped_query(base, key_rank, 4.0, 1.5)


def draw_w_cross_query(key, part):
    key = jax.random.fold_in(key, 23)
    key_rank, key_base = jax.random.split(key)
    base = jnp.clip(jax.random.normal(key_base, (D, H * DH), jnp.float32), -4.0, 4.0)
    return shaped_query(base, key_rank, 4.0, 1.5)


def plant(values, own_key, least, high):
    longest = values.shape.index(max(values.shape))
    spots = []
    for shift in (0, 1):
        where = [jax.random.randint(jax.random.fold_in(own_key, axis), (), 0, length) for axis, length in enumerate(values.shape)]
        where[longest] = (where[longest] + shift) % values.shape[longest]
        spots.append(tuple(where))
    return values.at[spots[0]].set(least).at[spots[1]].set(high)


def block_levels(rng, shape, pieces, smallest, high):
    def one(dim, parts):
        heights = jax.random.uniform(jax.random.fold_in(jax.random.fold_in(rng, 6), dim), (parts,), jnp.float32, smallest / len(pieces), high / len(pieces))
        return jnp.repeat(jnp.exp(heights), shape[dim] // parts).reshape((-1,) + (1,) * (len(shape) - dim - 1))

    level = one(*pieces[0])
    for cut in pieces[1:]:
        level = level * one(*cut)
    return level


def cumulative_ranks(number_of, lean):
    weights = [(1 << 20) // math.isqrt(standing ** lean) + 1 for standing in range(1, number_of + 1)]
    scale = 1 + sum(weights) // (1 << 30)
    return np.cumsum(np.array([max(1, weight // scale) for weight in weights]))


def ranked(stream_key, shape, amount, slope):
    table = cumulative_ranks(amount, slope)
    pick = jax.random.randint(jax.random.fold_in(stream_key, 1), shape, 0, int(table[amount - 1]))
    standing = jnp.searchsorted(jnp.asarray(table, jnp.int32), pick, side="right")
    return jax.random.permutation(jax.random.fold_in(stream_key, 2), amount)[standing].astype(jnp.int32)


def gaussian(rng, extent, width, reach, pieces=(), held_as=jnp.bfloat16):
    loudness = block_levels(rng, extent, pieces, -0.22, 0.18) if pieces else 1.0
    array = jax.random.normal(rng, extent, jnp.float32) * width * loudness
    return jnp.minimum(jnp.maximum(array, -reach), reach).astype(held_as)


def setup_inputs(seed: int = 0, part: int = 0) -> dict:
    arg_keys = jax.random.split(jax.random.key(seed), 19)
    own_keys = jax.random.split(jax.random.fold_in(arg_keys[18], part), 19)
    token_ids = plant(ranked(own_keys[0], (STEPS,), VOCAB, 2), jax.random.fold_in(own_keys[0], 3), 0, VOCAB - 1).astype(jnp.int32)
    embedding = gaussian(arg_keys[1], (VOCAB, D), 1.0, 6.0, ((0, 128),))
    passages = gaussian(own_keys[2], (NTOK, D), 1.0, 6.0, ((0, 16), (1, 8)))
    passage_lengths = plant(jax.random.randint(own_keys[3], (PASS,), PLEN // 8, PLEN + 1), jax.random.fold_in(own_keys[3], 1), PLEN // 8, PLEN).astype(jnp.int32)
    w_key = gaussian(arg_keys[4], (D, H * DH), D ** -0.5, 0.09375, ((0, 16), (1, 8)))
    w_value = gaussian(arg_keys[5], (D, H * DH), D ** -0.5, 0.09375, ((0, 16), (1, 8)))
    norm_self = jnp.clip(1.0 + 0.18 * jax.random.normal(arg_keys[6], (D,), jnp.float32), 0.1, 1.9)
    w_self_query = draw_w_self_query(jax.random.fold_in(arg_keys[18], 71), part)
    w_self_key = gaussian(arg_keys[8], (D, H * DH), D ** -0.5, 0.09375, ((0, 16), (1, 8)))
    w_self_value = gaussian(arg_keys[9], (D, H * DH), D ** -0.5, 0.09375, ((0, 16), (1, 8)))
    w_self_out = gaussian(arg_keys[10], (H * DH, D), (H * DH) ** -0.5, 0.09375, ((0, 8), (1, 16)))
    norm_cross = jnp.clip(1.0 + 0.18 * jax.random.normal(arg_keys[11], (D,), jnp.float32), 0.1, 1.9)
    w_cross_query = draw_w_cross_query(jax.random.fold_in(arg_keys[18], 71), part)
    w_cross_out = gaussian(arg_keys[13], (H * DH, D), (H * DH) ** -0.5, 0.09375, ((0, 8), (1, 16)))
    norm_ffn = jnp.clip(1.0 + 0.18 * jax.random.normal(arg_keys[14], (D,), jnp.float32), 0.1, 1.9)
    w_gate = gaussian(arg_keys[15], (D, FF), D ** -0.5, 0.09375, ((0, 16), (1, 8)))
    w_up = gaussian(arg_keys[16], (D, FF), D ** -0.5, 0.09375, ((0, 16), (1, 8)))
    w_down = gaussian(arg_keys[17], (FF, D), FF ** -0.5, 0.0625, ((0, 8), (1, 16)))
    return dict(token_ids=token_ids, embedding=embedding, passages=passages, passage_lengths=passage_lengths, w_key=w_key, w_value=w_value, norm_self=norm_self, w_self_query=w_self_query, w_self_key=w_self_key, w_self_value=w_self_value, w_self_out=w_self_out, norm_cross=norm_cross, w_cross_query=w_cross_query, w_cross_out=w_cross_out, norm_ffn=norm_ffn, w_gate=w_gate, w_up=w_up, w_down=w_down)


def rms_norm(state, gain):
    mean_sq = lax.optimization_barrier(jnp.mean(state * state, axis=-1, keepdims=True))
    return (state * jax.lax.rsqrt(mean_sq + 1e-06) * gain).astype(jnp.bfloat16)

def reference(token_ids, embedding, passages, passage_lengths, w_key, w_value, norm_self, w_self_query, w_self_key, w_self_value, w_self_out, norm_cross, w_cross_query, w_cross_out, norm_ffn, w_gate, w_up, w_down):
    scale = 1.0 / DH ** 0.5
    cross_keys = jnp.dot(passages, w_key, preferred_element_type=jnp.float32).astype(jnp.bfloat16)
    cross_values = jnp.dot(passages, w_value, preferred_element_type=jnp.float32).astype(jnp.bfloat16)
    state = embedding[token_ids].astype(jnp.float32)
    normed = rms_norm(state, norm_self)
    query = jnp.dot(normed, w_self_query, preferred_element_type=jnp.float32).astype(jnp.bfloat16).reshape(STEPS, H, DH)
    keyed = jnp.dot(normed, w_self_key, preferred_element_type=jnp.float32).astype(jnp.bfloat16).reshape(STEPS, H, DH)
    valued = jnp.dot(normed, w_self_value, preferred_element_type=jnp.float32).astype(jnp.bfloat16).reshape(STEPS, H, DH)
    scores = jnp.einsum('shd,rhd->hsr', query.astype(jnp.float32), keyed.astype(jnp.float32)) * scale
    causal = jnp.arange(STEPS)[:, None] >= jnp.arange(STEPS)[None, :]
    scores = jnp.where(causal[None], scores, -1e+30)
    peak = lax.optimization_barrier(jnp.max(scores, axis=-1, keepdims=True))
    weights = jnp.where(causal[None], jnp.exp(scores - peak), 0.0).astype(jnp.bfloat16).astype(jnp.float32)
    total = lax.optimization_barrier(jnp.sum(weights, axis=-1))
    mixed = jnp.einsum('hsr,rhd->hsd', weights, valued.astype(jnp.float32)) / total[..., None]
    self_heads = jnp.transpose(mixed, (1, 0, 2)).astype(jnp.bfloat16).reshape(STEPS, H * DH)
    state = state + jnp.dot(self_heads, w_self_out, preferred_element_type=jnp.float32)
    normed = rms_norm(state, norm_cross)
    cquery = jnp.dot(normed, w_cross_query, preferred_element_type=jnp.float32).astype(jnp.bfloat16).reshape(STEPS, H, DH)
    ckeys = cross_keys.reshape(NTOK, H, DH).astype(jnp.float32)
    cvalues = cross_values.reshape(NTOK, H, DH).astype(jnp.float32)
    cscores = jnp.einsum('shd,nhd->hsn', cquery.astype(jnp.float32), ckeys) * scale
    live = (jnp.arange(PLEN)[None, :] < passage_lengths[:, None]).reshape(NTOK)
    cscores = jnp.where(live[None, None], cscores, -1e+30)
    cpeak = lax.optimization_barrier(jnp.max(cscores, axis=-1, keepdims=True))
    cweights = jnp.where(live[None, None], jnp.exp(cscores - cpeak), 0.0).astype(jnp.bfloat16).astype(jnp.float32)
    ctotal = lax.optimization_barrier(jnp.sum(cweights, axis=-1))
    cmixed = jnp.einsum('hsn,nhd->hsd', cweights, cvalues) / ctotal[..., None]
    cross_heads = jnp.transpose(cmixed, (1, 0, 2)).astype(jnp.bfloat16).reshape(STEPS, H * DH)
    state = state + jnp.dot(cross_heads, w_cross_out, preferred_element_type=jnp.float32)
    normed = rms_norm(state, norm_ffn)
    gated = jnp.dot(normed, w_gate, preferred_element_type=jnp.float32)
    upper = jnp.dot(normed, w_up, preferred_element_type=jnp.float32)
    hidden = (jax.nn.gelu(gated, approximate=True) * upper).astype(jnp.bfloat16)
    layer_out = state + jnp.dot(hidden, w_down, preferred_element_type=jnp.float32)
    return (layer_out, cross_keys, cross_values)
```

```python
import jax
import jax.numpy as jnp
from jax import lax
from jax.experimental import pallas as pl
from jax.experimental.pallas import tpu as pltpu
from jax.sharding import PartitionSpec as P

BF = jnp.bfloat16
F32 = jnp.float32
MESH = pl.DeviceIdType.MESH
D = 4096
DH = 64
PLEN = 256
STEPS = 4
ROWS = 512
COLS = 512
OWN = 256
FFC = 1280
VROWS = 251
ACH = 4
WCH = 2
ARO = ROWS // ACH
WRO = OWN // WCH


def pack8(v):
    n = v.shape[1] // 2
    return jnp.concatenate([v[:, :n], v[:, n:]], axis=0)


def unpack8(p):
    return jnp.concatenate([p[:4], p[4:8]], axis=1)


def pack16(v):
    n = v.shape[1] // 4
    return jnp.concatenate([v[:, n * k : n * k + n] for k in range(4)], axis=0)


def unpack16(p):
    return jnp.concatenate([p[4 * k : 4 * k + 4] for k in range(4)], axis=1)


def pad8(v):
    return jnp.concatenate([v, jnp.zeros_like(v)], axis=0)


def head_mask():
    head = lax.broadcasted_iota(jnp.int32, (8, COLS), 0)
    lane = lax.broadcasted_iota(jnp.int32, (8, COLS), 1)
    return jnp.where((lane >= head * DH) & (lane < head * DH + DH), 1.0, 0.0).astype(F32)


def by_head(q):
    mask = head_mask()
    return jnp.concatenate([q[s : s + 1] * mask for s in range(STEPS)], axis=0).astype(BF)


def own_head(acc):
    mask = head_mask()
    rows = [
        jnp.sum(acc[8 * s : 8 * s + 8] * mask, axis=0, keepdims=True) for s in range(STEPS)
    ]
    return jnp.concatenate(rows, axis=0)


def attend(q, keys, values, live):
    scores = lax.dot_general(
        by_head(q), keys, (((1,), (1,)), ((), ())), preferred_element_type=F32
    ) * (1.0 / DH**0.5)
    scores = jnp.where(live, scores, -1e30)
    peak = jnp.max(scores, axis=1, keepdims=True)
    weights = jnp.where(live, jnp.exp(scores - peak), 0.0).astype(BF)
    total = jnp.sum(weights.astype(F32), axis=1, keepdims=True)
    accum = jnp.dot(weights, values, preferred_element_type=F32)
    return peak, total, accum


def split_sum(ss):
    hi = ss.astype(BF).astype(F32)
    lo = ss - hi
    z = jnp.zeros_like(ss)
    return jnp.broadcast_to(jnp.concatenate([hi, lo, z, z], axis=0), (16, 128))


def kernel(
    tok,
    lens,
    g_self,
    g_cross,
    g_ffn,
    passages,
    w_key,
    w_value,
    w_sq,
    w_sk,
    w_sv,
    w_so,
    w_cq,
    w_co,
    w_gate,
    w_up,
    w_down,
    emb,
    out,
    kout,
    vout,
    a_all,
    w_all,
    kv,
    emb_v,
    sq_v,
    sk_v,
    sv_v,
    so_v,
    cq_v,
    co_v,
    gate_v,
    up_v,
    down_v,
    s1a,
    r1a,
    r1b,
    r2,
    r3,
    r4,
    r5,
    r6,
    r7,
    r8,
    lsem,
    osem,
    az_r,
    ay_r,
    wz_r,
    wx_r,
    ws_r,
    big_s,
    es,
    er,
):
    pb = lax.axis_index("pb")
    pas = lax.axis_index("pas")
    tp = lax.axis_index("tp")
    x, zl = pas // 4, pas % 4
    zh, y = tp // 4, tp % 4
    xs = [(x + k) % 4 for k in range(4)]
    zs = [(zl + k) % 4 for k in range(4)]
    ys = [(y + k) % 4 for k in range(4)]
    xb = [(x - k + 4) % 4 for k in range(4)]
    zb = [(zl - k + 4) % 4 for k in range(4)]
    far = (2, 1, 3, 0)
    pas_peers = [
        (pb, xs[a] * 4 + zs[b], tp) for a in far for b in (3, 2, 1, 0) if (a, b) != (0, 0)
    ]
    tp_peers = [
        (pb, pas, (zh * 4 if b == 0 else (1 - zh) * 4) + ys[a])
        for b in (1, 0)
        for a in far
        if (a, b) != (0, 0)
    ]
    x_peers = {k: (pb, xs[k] * 4 + zl, tp) for k in (1, 3, 2)}
    z_peers = {k: (pb, x * 4 + zs[k], tp) for k in (1, 3, 2)}
    y_peers = {k: (pb, pas, zh * 4 + ys[k]) for k in (1, 3, 2)}
    z4_peer = (pb, pas, (1 - zh) * 4 + y)
    sibling = (1 - pb, pas, tp)

    pas0 = pl.multiple_of(pas * OWN, OWN)
    tp0 = pl.multiple_of(tp * COLS, COLS)
    loads = [
        (passages, a_all.at[:, pl.ds(tp0, COLS)]),
        (w_key, w_all.at[0, pl.ds(pas0, OWN)]),
        (w_value, w_all.at[1, pl.ds(pas0, OWN)]),
        (emb, emb_v),
        (w_sq, sq_v),
        (w_sk, sk_v),
        (w_sv, sv_v),
        (w_so, so_v),
        (w_cq, cq_v),
        (w_co, co_v),
        (w_gate, gate_v),
        (w_up, up_v),
        (w_down, down_v),
    ]
    local = [pltpu.make_async_copy(s, d, lsem.at[n]) for n, (s, d) in enumerate(loads)]
    for c in local:
        c.start()

    barrier = pltpu.get_barrier_semaphore()
    greet = pas_peers + tp_peers + [sibling]
    for d in greet:
        pl.semaphore_signal(barrier, inc=1, device_id=d, device_id_type=MESH)
    pl.semaphore_wait(barrier, len(greet))

    def send(src, dst, ssem, rsem, dev):
        pltpu.make_async_remote_copy(
            src_ref=src,
            dst_ref=dst,
            send_sem=ssem,
            recv_sem=rsem,
            device_id=dev,
            device_id_type=MESH,
        ).start()

    def wait_bytes(ref, sem):
        pltpu.make_async_copy(ref, ref, sem).wait()

    def a_piece(block, c):
        cols = pl.ds(pl.multiple_of(block * COLS, COLS), COLS)
        return a_all.at[pl.ds(c * ARO, ARO), cols]

    def w_piece(block, c):
        return w_all.at[pb, pl.ds(pl.multiple_of(block * OWN + c * WRO, WRO), WRO)]

    def a_send(block, c, peers, rsem):
        piece = a_piece(block, c)
        for p in peers:
            send(piece, piece, big_s.at[0], rsem, p)

    def w_sibling(block, c):
        piece = w_piece(block, c)
        send(piece, piece, big_s.at[2], ws_r.at[0], sibling)

    def w_to_x(block, kz, c):
        piece = w_piece(block, c)
        for k in (1, 3, 2):
            send(piece, piece, big_s.at[1], wx_r.at[k - 1, kz, c], x_peers[k])

    def w_from_z(kz):
        block = x * 4 + zb[kz]
        for c in range(WCH):
            wait_bytes(w_piece(block, c), wz_r.at[kz - 1, c])
            w_to_x(block, kz, c)
            w_sibling(block, c)

    def w_from_x(kx, kz):
        block = xb[kx] * 4 + zb[kz]
        for c in range(WCH):
            wait_bytes(w_piece(block, c), wx_r.at[kx - 1, kz, c])
            w_sibling(block, c)

    def a_from_z(c):
        block = (1 - zh) * 4 + y
        wait_bytes(a_piece(block, c), az_r.at[c])
        a_send(block, c, [y_peers[k] for k in (1, 3, 2)], ay_r.at[1])

    def spread(buf, me, peers, n):
        slot = buf.at[me]
        for p in peers:
            send(slot, slot, es.at[n], er.at[n], p)

    def collect(buf, count, n):
        wait_bytes(buf.at[pl.ds(0, count - 1)], er.at[n])

    def gain(g):
        return jnp.concatenate([g[pl.ds(2 * pas, 1), :], g[pl.ds(2 * pas + 1, 1), :]], axis=1)

    for n in range(3):
        local[n].wait()
    for c in range(WCH):
        piece = w_piece(pas, c)
        for k in (1, 3, 2):
            send(piece, piece, big_s.at[1], wz_r.at[k - 1, c], z_peers[k])
        w_to_x(pas, 0, c)
    for c in range(ACH):
        a_send(tp, c, [z4_peer], az_r.at[c])
        a_send(tp, c, [y_peers[k] for k in (1, 3, 2)], ay_r.at[0])

    local[3].wait()
    row = lax.broadcasted_iota(jnp.int32, (8, VROWS), 0)
    place = lax.broadcasted_iota(jnp.int32, (8, VROWS), 1) + (pas * 8 + tp) * VROWS
    wanted = jnp.full((8, VROWS), -1, jnp.int32)
    for s in range(STEPS):
        wanted = jnp.where(row == s, tok[s], wanted)
    onehot = jnp.where(place == wanted, 1.0, 0.0).astype(BF)
    mine = jnp.dot(onehot, emb_v[...], preferred_element_type=F32)
    for i in range(16):
        s1a[i] = pack8(mine[:4, OWN * i : OWN * i + OWN])
    r1a[pas] = s1a[pas]
    for p in pas_peers:
        send(s1a.at[p[1]], r1a.at[pas], es.at[0], er.at[0], p)

    w_from_z(1)

    collect(r1a, 16, 0)
    r1b[tp] = jnp.sum(r1a[...], axis=0)
    spread(r1b, tp, tp_peers, 1)

    w_from_z(3)
    a_from_z(0)

    collect(r1b, 8, 1)
    state0 = unpack8(jnp.sum(r1b[...], axis=0))

    def scaled(state, g):
        ss = jnp.sum(state * state, axis=1, keepdims=True)
        return pad8(state * gain(g)).astype(BF), ss

    def rms(ss):
        return lax.rsqrt(ss * (1.0 / D) + 1e-06)

    a, ss = scaled(state0, g_self)
    parts = []
    for n, w in ((4, sq_v), (5, sk_v), (6, sv_v)):
        local[n].wait()
        parts.append(pack16(jnp.dot(a, w[...], preferred_element_type=F32)[:4]))
    r2[pas] = jnp.concatenate(parts + [split_sum(ss)], axis=1).astype(BF)
    spread(r2, pas, pas_peers, 2)

    w_from_z(2)
    a_from_z(1)

    collect(r2, 16, 2)
    total = r2[0].astype(F32)
    for i in range(1, 16):
        total = total + r2[i].astype(F32)
    scale = rms(total[0:4, 384:385] + total[4:8, 384:385])
    q, k, v = [unpack16(total[:, 128 * n : 128 * n + 128]) * scale for n in range(3)]
    none = jnp.zeros((124, COLS), F32)
    keys = jnp.concatenate([k, none], axis=0).astype(BF)
    values = jnp.concatenate([v, none], axis=0).astype(BF)
    step = lax.broadcasted_iota(jnp.int32, (32, 128), 0)
    other = lax.broadcasted_iota(jnp.int32, (32, 128), 1)
    _, weight, accum = attend(q.astype(BF).astype(F32), keys, values, other * 8 <= step)
    heads = own_head(accum / weight)
    local[7].wait()
    r3[tp] = pack8(jnp.dot(pad8(heads).astype(BF), so_v[...], preferred_element_type=F32)[:4])
    spread(r3, tp, tp_peers, 3)

    a_from_z(2)
    for kx in (1, 3, 2):
        w_from_x(kx, 0)

    collect(r3, 8, 3)
    state1 = state0 + unpack8(jnp.sum(r3[...], axis=0))
    a, ss = scaled(state1, g_cross)
    local[8].wait()
    part = jnp.dot(a, cq_v[...], preferred_element_type=F32)[:4]
    r4[pas] = jnp.concatenate([pack8(part), jnp.broadcast_to(pad8(ss), (8, 128))], axis=1)
    spread(r4, pas, pas_peers, 4)

    a_from_z(3)
    for kz in (1, 3, 2):
        for kx in (1, 3, 2):
            w_from_x(kx, kz)

    collect(r4, 16, 4)
    total = jnp.sum(r4[...], axis=0)
    cquery = unpack8(total[:, :256]) * rms(total[:4, 256:257])

    wait_bytes(a_all.at[:, pl.ds(0, 3 * COLS)], ay_r.at[0])
    wait_bytes(a_all.at[:, pl.ds(0, 3 * COLS)], ay_r.at[1])
    wait_bytes(w_all.at[0, pl.ds(0, 15 * OWN)], ws_r.at[0])
    for c in range(2):

        def tile(n, carry):
            cols = pl.ds(pl.multiple_of(n * 256, 256), 256)
            kv[c, :, cols] = jnp.dot(
                a_all[...], w_all[c, :, cols], preferred_element_type=F32
            ).astype(BF)
            return carry

        lax.fori_loop(0, 2, tile, 0)
    outs = [
        pltpu.make_async_copy(kv.at[0], kout, osem.at[0]),
        pltpu.make_async_copy(kv.at[1], vout, osem.at[1]),
    ]
    for c in outs:
        c.start()

    slot = lax.broadcasted_iota(jnp.int32, (32, ROWS), 1)
    live = (slot < lens[0]) | ((slot >= PLEN) & (slot < lens[1] + PLEN))
    peak, weight, accum = attend(cquery.astype(BF).astype(F32), kv[0], kv[1], live)
    head = lax.broadcasted_iota(jnp.int32, (8, 128), 0)
    lane = lax.broadcasted_iota(jnp.int32, (8, 128), 1)
    rows = []
    for g in range(2):
        for s in range(STEPS):
            both = jnp.where(lane == head - 4 * g, peak[8 * s : 8 * s + 8], 0.0) + jnp.where(
                (lane >= 64) & (lane - 64 == head - 4 * g), weight[8 * s : 8 * s + 8], 0.0
            )
            rows.append(jnp.sum(both, axis=0, keepdims=True))
    r5[pas] = jnp.concatenate([pack8(own_head(accum)), jnp.concatenate(rows, axis=0)], axis=1)
    spread(r5, pas, pas_peers, 5)
    collect(r5, 16, 5)
    peaks = [r5[i, :, 256:384] for i in range(16)]
    top = peaks[0]
    for i in range(1, 16):
        top = jnp.maximum(top, peaks[i])
    shares = []
    weight = jnp.zeros((8, 128), F32)
    for i in range(16):
        share = jnp.where(lane < 4, jnp.exp(peaks[i] - top), 0.0)
        weight = weight + share * pltpu.roll(peaks[i], 64, 1)
        shares.append(share)
    inv = 1.0 / jnp.where(lane < 4, weight, 1.0)
    shares = jnp.concatenate([s * inv for s in shares], axis=0)
    lane_of = lax.broadcasted_iota(jnp.int32, (128, 256), 0)
    column = lax.broadcasted_iota(jnp.int32, (128, 256), 1)
    widen = jnp.where((column >= lane_of * DH) & (column < lane_of * DH + DH), 1.0, 0.0)
    wide = jnp.dot(
        shares, widen.astype(F32), preferred_element_type=F32, precision=lax.Precision.HIGHEST
    )
    mixed = jnp.zeros((8, 256), F32)
    for i in range(16):
        mixed = mixed + wide[8 * i : 8 * i + 8] * r5[i, :, :256]
    local[9].wait()
    heads = pad8(unpack8(mixed)).astype(BF)
    r6[tp] = pack8(jnp.dot(heads, co_v[...], preferred_element_type=F32)[:4])
    spread(r6, tp, tp_peers, 6)
    collect(r6, 8, 6)
    state2 = state1 + unpack8(jnp.sum(r6[...], axis=0))

    a, ss = scaled(state2, g_ffn)
    local[10].wait()
    local[11].wait()
    gated = jnp.dot(a, gate_v[...], preferred_element_type=F32)[:4]
    upper = jnp.dot(a, up_v[...], preferred_element_type=F32)[:4]
    r7[pas] = jnp.concatenate(
        [pack16(jnp.concatenate([gated, upper], axis=1)), split_sum(ss)], axis=1
    ).astype(BF)
    spread(r7, pas, pas_peers, 7)
    collect(r7, 16, 7)
    total = r7[0].astype(F32)
    for i in range(1, 16):
        total = total + r7[i].astype(F32)
    scale = rms(total[0:4, 640:641] + total[4:8, 640:641])
    scale = jnp.concatenate([scale, scale], axis=0)
    gated = total[0:8, :640] * scale
    upper = total[8:16, :640] * scale
    gelu = 0.5 * gated * (1.0 + jnp.tanh(0.7978845608028654 * (gated + 0.044715 * gated * gated * gated)))
    hidden = (gelu * upper).astype(BF)
    local[12].wait()
    low = jnp.dot(hidden, down_v[0:640], preferred_element_type=F32)
    high = jnp.dot(hidden, down_v[640:1280], preferred_element_type=F32)
    r8[tp] = pack8(low[:4] + high[4:8])
    spread(r8, tp, tp_peers, 8)
    collect(r8, 8, 8)
    whole = state2 + unpack8(jnp.sum(r8[...], axis=0))
    own = whole[:, 0:32]
    for t in range(1, 8):
        own = jnp.where(tp == t, whole[:, 32 * t : 32 * t + 32], own)
    out[...] = own

    for n, (buf, count) in enumerate(
        ((r1a, 16), (r1b, 8), (r2, 16), (r3, 8), (r4, 16), (r5, 16), (r6, 8), (r7, 16), (r8, 8))
    ):
        wait_bytes(buf.at[pl.ds(0, count - 1)], es.at[n])
    wait_bytes(a_all.at[:, pl.ds(0, 7 * COLS)], big_s.at[0])
    wait_bytes(w_all.at[0, pl.ds(0, 15 * OWN)], big_s.at[1])
    wait_bytes(w_all.at[0, pl.ds(0, 15 * OWN)], big_s.at[2])
    for c in outs:
        c.wait()


def shards(
    token_ids,
    embedding,
    passages,
    passage_lengths,
    w_key,
    w_value,
    norm_self,
    w_self_query,
    w_self_key,
    w_self_value,
    w_self_out,
    norm_cross,
    w_cross_query,
    w_cross_out,
    norm_ffn,
    w_gate,
    w_up,
    w_down,
):
    smem = pl.BlockSpec(memory_space=pltpu.SMEM)
    vmem = pl.BlockSpec(memory_space=pltpu.VMEM)
    hbm = pl.BlockSpec(memory_space=pltpu.HBM)
    dma = pltpu.SemaphoreType.DMA
    return pl.pallas_call(
        kernel,
        name="decoder_layer",
        out_shape=(
            jax.ShapeDtypeStruct((STEPS, 32), F32),
            jax.ShapeDtypeStruct((ROWS, COLS), BF),
            jax.ShapeDtypeStruct((ROWS, COLS), BF),
        ),
        in_specs=[smem, smem, vmem, vmem, vmem] + [hbm] * 13,
        out_specs=(vmem, hbm, hbm),
        scratch_shapes=[
            pltpu.VMEM((ROWS, D), BF),
            pltpu.VMEM((2, D, COLS), BF),
            pltpu.VMEM((2, ROWS, COLS), BF),
            pltpu.VMEM((VROWS, D), BF),
            pltpu.VMEM((OWN, COLS), BF),
            pltpu.VMEM((OWN, COLS), BF),
            pltpu.VMEM((OWN, COLS), BF),
            pltpu.VMEM((COLS, OWN), BF),
            pltpu.VMEM((OWN, COLS), BF),
            pltpu.VMEM((COLS, OWN), BF),
            pltpu.VMEM((OWN, FFC), BF),
            pltpu.VMEM((OWN, FFC), BF),
            pltpu.VMEM((FFC, OWN), BF),
            pltpu.VMEM((16, 8, 128), F32),
            pltpu.VMEM((16, 8, 128), F32),
            pltpu.VMEM((8, 8, 128), F32),
            pltpu.VMEM((16, 16, 512), BF),
            pltpu.VMEM((8, 8, 128), F32),
            pltpu.VMEM((16, 8, 384), F32),
            pltpu.VMEM((16, 8, 384), F32),
            pltpu.VMEM((8, 8, 128), F32),
            pltpu.VMEM((16, 16, 768), BF),
            pltpu.VMEM((8, 8, 128), F32),
            dma((13,)),
            dma((2,)),
            dma((ACH,)),
            dma((2,)),
            dma((3, WCH)),
            dma((3, 4, WCH)),
            dma((1,)),
            dma((3,)),
            dma((9,)),
            dma((9,)),
        ],
        compiler_params=pltpu.CompilerParams(
            collective_id=1, has_side_effects=True, vmem_limit_bytes=56 << 20
        ),
        cost_estimate=pl.CostEstimate(
            flops=2 * 2 * ROWS * COLS * D, bytes_accessed=16 << 20, transcendentals=1 << 20
        ),
    )(
        token_ids,
        passage_lengths,
        norm_self.reshape(32, 128),
        norm_cross.reshape(32, 128),
        norm_ffn.reshape(32, 128),
        passages,
        w_key,
        w_value,
        w_self_query,
        w_self_key,
        w_self_value,
        w_self_out,
        w_cross_query,
        w_cross_out,
        w_gate,
        w_up,
        w_down,
        embedding,
    )


def solution(mesh):
    in_specs = (
        P("pb"),
        P(("pas", "tp"), None),
        P(("pb", "pas"), "tp"),
        P(("pb", "pas")),
        P("pas", "tp"),
        P("pas", "tp"),
        P(),
        P("pas", "tp"),
        P("pas", "tp"),
        P("pas", "tp"),
        P("tp", "pas"),
        P(),
        P("pas", "tp"),
        P("tp", "pas"),
        P(),
        P("pas", "tp"),
        P("pas", "tp"),
        P("tp", "pas"),
    )
    out_specs = (P("pb", ("pas", "tp")), P(("pb", "pas"), "tp"), P(("pb", "pas"), "tp"))
    return jax.shard_map(shards, mesh=mesh, in_specs=in_specs, out_specs=out_specs, check_vma=False)
```

```python
import jax
import jax.numpy as jnp
from jax import lax
from jax.experimental import pallas as pl
from jax.experimental.pallas import tpu as pltpu
from jax.sharding import PartitionSpec as P

BF = jnp.bfloat16
F32 = jnp.float32
MESH = pl.DeviceIdType.MESH
D = 4096
DH = 64
PLEN = 256
STEPS = 4
ROWS = 512
COLS = 512
OWN = 256
FFC = 1280
VROWS = 251
ACH = 4
WCH = 2
ARO = ROWS // ACH
WRO = OWN // WCH
PASSED = ((1, 0), (3, 1))
KEPT = ((1, 1), (3, 0), (2, 0), (2, 1))


def pack8(v):
    n = v.shape[1] // 2
    return jnp.concatenate([v[:, :n], v[:, n:]], axis=0)


def unpack8(p):
    return jnp.concatenate([p[:4], p[4:8]], axis=1)


def pack16(v):
    n = v.shape[1] // 4
    return jnp.concatenate([v[:, n * k : n * k + n] for k in range(4)], axis=0)


def unpack16(p):
    return jnp.concatenate([p[4 * k : 4 * k + 4] for k in range(4)], axis=1)


def pad8(v):
    return jnp.concatenate([v, jnp.zeros_like(v)], axis=0)


def head_mask():
    head = lax.broadcasted_iota(jnp.int32, (8, COLS), 0)
    lane = lax.broadcasted_iota(jnp.int32, (8, COLS), 1)
    return jnp.where((lane >= head * DH) & (lane < head * DH + DH), 1.0, 0.0).astype(F32)


def by_head(q):
    mask = head_mask()
    return jnp.concatenate([q[s : s + 1] * mask for s in range(STEPS)], axis=0).astype(BF)


def own_head(acc):
    mask = head_mask()
    rows = [
        jnp.sum(acc[8 * s : 8 * s + 8] * mask, axis=0, keepdims=True) for s in range(STEPS)
    ]
    return jnp.concatenate(rows, axis=0)


def attend(q, keys, values, live):
    scores = lax.dot_general(
        by_head(q), keys, (((1,), (1,)), ((), ())), preferred_element_type=F32
    ) * (1.0 / DH**0.5)
    scores = jnp.where(live, scores, -1e30)
    peak = jnp.max(scores, axis=1, keepdims=True)
    weights = jnp.where(live, jnp.exp(scores - peak), 0.0).astype(BF)
    total = jnp.sum(weights.astype(F32), axis=1, keepdims=True)
    accum = jnp.dot(weights, values, preferred_element_type=F32)
    return peak, total, accum


def split_sum(ss):
    hi = ss.astype(BF).astype(F32)
    lo = ss - hi
    z = jnp.zeros_like(ss)
    return jnp.broadcast_to(jnp.concatenate([hi, lo, z, z], axis=0), (16, 128))


def kernel(
    tok,
    lens,
    g_self,
    g_cross,
    g_ffn,
    passages,
    w_key,
    w_value,
    w_sq,
    w_sk,
    w_sv,
    w_so,
    w_cq,
    w_co,
    w_gate,
    w_up,
    w_down,
    emb,
    out,
    kout,
    vout,
    a_all,
    w_all,
    kv,
    emb_v,
    sq_v,
    sk_v,
    sv_v,
    so_v,
    cq_v,
    co_v,
    gate_v,
    up_v,
    down_v,
    s1a,
    r1a,
    r1b,
    r2,
    r2z,
    r3,
    r4,
    r4z,
    r5,
    r6,
    r7,
    r8,
    lsem,
    osem,
    az_r,
    af_r,
    an_r,
    wz_r,
    wx_r,
    ws_r,
    big_s,
    es,
    er,
):
    pb = lax.axis_index("pb")
    pas = lax.axis_index("pas")
    tp = lax.axis_index("tp")
    x, zl = pas // 4, pas % 4
    zh, y = tp // 4, tp % 4
    xs = [(x + k) % 4 for k in range(4)]
    zs = [(zl + k) % 4 for k in range(4)]
    ys = [(y + k) % 4 for k in range(4)]
    xb = [(x - k + 4) % 4 for k in range(4)]
    zb = [(zl - k + 4) % 4 for k in range(4)]
    yb = [(y - k + 4) % 4 for k in range(4)]
    far = (2, 1, 3, 0)
    pas_peers = [
        (pb, xs[a] * 4 + zs[b], tp) for a in far for b in (3, 2, 1, 0) if (a, b) != (0, 0)
    ]
    tp_peers = [
        (pb, pas, (zh * 4 if b == 0 else (1 - zh) * 4) + ys[a])
        for b in (1, 0)
        for a in far
        if (a, b) != (0, 0)
    ]
    x_peers = {k: (pb, xs[k] * 4 + zl, tp) for k in (1, 3, 2)}
    z_peers = {k: (pb, x * 4 + zs[k], tp) for k in (1, 3, 2)}
    y_peers = {k: (pb, pas, zh * 4 + ys[k]) for k in (1, 3, 2)}
    z4_peer = (pb, pas, (1 - zh) * 4 + y)
    sibling = (1 - pb, pas, tp)

    pas0 = pl.multiple_of(pas * OWN, OWN)
    tp0 = pl.multiple_of(tp * COLS, COLS)
    loads = [
        (passages, a_all.at[:, pl.ds(tp0, COLS)]),
        (w_key, w_all.at[0, pl.ds(pas0, OWN)]),
        (w_value, w_all.at[1, pl.ds(pas0, OWN)]),
        (emb, emb_v),
        (w_sq, sq_v),
        (w_sk, sk_v),
        (w_sv, sv_v),
        (w_so, so_v),
        (w_cq, cq_v),
        (w_co, co_v),
        (w_gate, gate_v),
        (w_up, up_v),
        (w_down, down_v),
    ]
    local = [pltpu.make_async_copy(s, d, lsem.at[n]) for n, (s, d) in enumerate(loads)]
    for c in local:
        c.start()

    barrier = pltpu.get_barrier_semaphore()
    greet = pas_peers + tp_peers + [sibling]
    for d in greet:
        pl.semaphore_signal(barrier, inc=1, device_id=d, device_id_type=MESH)

    def send(src, dst, ssem, rsem, dev):
        pltpu.make_async_remote_copy(
            src_ref=src,
            dst_ref=dst,
            send_sem=ssem,
            recv_sem=rsem,
            device_id=dev,
            device_id_type=MESH,
        ).start()

    def wait_bytes(ref, sem):
        pltpu.make_async_copy(ref, ref, sem).wait()

    def a_piece(block, c):
        cols = pl.ds(pl.multiple_of(block * COLS, COLS), COLS)
        return a_all.at[pl.ds(c * ARO, ARO), cols]

    def w_piece(block, c):
        return w_all.at[pb, pl.ds(pl.multiple_of(block * OWN + c * WRO, WRO), WRO)]

    def a_to_z(c):
        piece = a_piece(tp, c)
        send(piece, piece, big_s.at[0], az_r.at[c], z4_peer)

    def a_to_y(half, block, c):
        piece = a_piece(block, c)
        for k, passed_on in ((1, c % 2 == 0), (3, c % 2 == 1)):
            rsem = af_r.at[half, c] if passed_on else an_r.at[half]
            send(piece, piece, big_s.at[0], rsem, y_peers[k])

    def a_from_z(c):
        block = (1 - zh) * 4 + y
        wait_bytes(a_piece(block, c), az_r.at[c])
        a_to_y(1, block, c)

    def a_from_y(half, c):
        k = 1 if c % 2 == 0 else 3
        block = (zh if half == 0 else 1 - zh) * 4 + yb[k]
        piece = a_piece(block, c)
        wait_bytes(piece, af_r.at[half, c])
        send(piece, piece, big_s.at[0], an_r.at[half], y_peers[k])

    def w_sibling(block, c):
        piece = w_piece(block, c)
        send(piece, piece, big_s.at[2], ws_r.at[0], sibling)

    def w_to_x(block, kz, c):
        piece = w_piece(block, c)
        for k in (1, 3):
            send(piece, piece, big_s.at[1], wx_r.at[k - 1, kz, c], x_peers[k])

    def w_to_z(k):
        for c in range(WCH):
            piece = w_piece(pas, c)
            send(piece, piece, big_s.at[1], wz_r.at[k - 1, c], z_peers[k])

    def w_from_z(kz):
        block = x * 4 + zb[kz]
        for c in range(WCH):
            wait_bytes(w_piece(block, c), wz_r.at[kz - 1, c])
            w_to_x(block, kz, c)
            w_sibling(block, c)

    def w_from_x(kz, pieces):
        for kx, c in pieces:
            block = xb[kx] * 4 + zb[kz]
            piece = w_piece(block, c)
            wait_bytes(piece, wx_r.at[kx - 1, kz, c])
            if (kx, c) in PASSED:
                send(piece, piece, big_s.at[1], wx_r.at[1, kz, c], x_peers[kx])
            w_sibling(block, c)

    def spread(buf, me, peers, n):
        slot = buf.at[me]
        for p in peers:
            send(slot, slot, es.at[n], er.at[n], p)

    def collect(buf, count, n):
        wait_bytes(buf.at[pl.ds(0, count - 1)], er.at[n])

    def merge_pas(part, bx, bz, n):
        bx[x] = part
        for k in (2, 1, 3):
            send(bx.at[x], bx.at[x], es.at[n], er.at[n], x_peers[k])

    def merge_pas_z(bx, bz, n):
        wait_bytes(bx.at[pl.ds(0, 3)], er.at[n])
        bz[zl] = bx[0] + bx[1] + bx[2] + bx[3]
        for k in (3, 2, 1):
            send(bz.at[zl], bz.at[zl], es.at[n + 7], er.at[n + 7], z_peers[k])

    def merged(bz, n):
        wait_bytes(bz.at[pl.ds(0, 3)], er.at[n + 7])
        return bz[0] + bz[1] + bz[2] + bz[3]

    def gain(g):
        return jnp.concatenate([g[pl.ds(2 * pas, 1), :], g[pl.ds(2 * pas + 1, 1), :]], axis=1)

    local[3].wait()
    row = lax.broadcasted_iota(jnp.int32, (8, VROWS), 0)
    place = lax.broadcasted_iota(jnp.int32, (8, VROWS), 1) + (pas * 8 + tp) * VROWS
    wanted = jnp.full((8, VROWS), -1, jnp.int32)
    for s in range(STEPS):
        wanted = jnp.where(row == s, tok[s], wanted)
    onehot = jnp.where(place == wanted, 1.0, 0.0).astype(BF)
    mine = jnp.dot(onehot, emb_v[...], preferred_element_type=F32)
    for i in range(16):
        s1a[i] = pack8(mine[:4, OWN * i : OWN * i + OWN])
    r1a[pas] = s1a[pas]
    pl.semaphore_wait(barrier, len(greet))
    for p in pas_peers:
        send(s1a.at[p[1]], r1a.at[pas], es.at[0], er.at[0], p)

    for n in range(3):
        local[n].wait()
    for c in range(WCH):
        w_to_x(pas, 0, c)
    w_to_z(1)
    a_to_z(0)
    for c in range(ACH):
        a_to_y(0, tp, c)

    w_from_x(0, PASSED)
    w_from_z(1)
    w_to_z(3)

    collect(r1a, 16, 0)
    r1b[tp] = jnp.sum(r1a[...], axis=0)
    spread(r1b, tp, tp_peers, 1)

    a_from_y(0, 0)
    a_from_y(0, 1)
    a_from_z(0)
    a_to_z(1)
    w_from_x(1, PASSED)
    w_from_x(0, KEPT)

    collect(r1b, 8, 1)
    state0 = unpack8(jnp.sum(r1b[...], axis=0))

    def scaled(state, g):
        ss = jnp.sum(state * state, axis=1, keepdims=True)
        return pad8(state * gain(g)).astype(BF), ss

    def rms(ss):
        return lax.rsqrt(ss * (1.0 / D) + 1e-06)

    a, ss = scaled(state0, g_self)
    parts = []
    for n, w in ((4, sq_v), (5, sk_v), (6, sv_v)):
        local[n].wait()
        parts.append(pack8(jnp.dot(a, w[...], preferred_element_type=F32)[:4]))
    parts.append(jnp.broadcast_to(pad8(ss), (8, 128)))
    merge_pas(jnp.concatenate(parts, axis=1), r2, r2z, 2)

    a_from_y(0, 2)
    a_from_y(0, 3)
    w_from_z(3)
    w_to_z(2)
    merge_pas_z(r2, r2z, 2)

    a_from_y(1, 0)
    a_from_z(1)
    a_to_z(2)
    w_from_x(3, PASSED)
    w_from_x(1, KEPT)

    total = merged(r2z, 2)
    scale = rms(total[:4, 768:769])
    q, k, v = [unpack8(total[:, 256 * n : 256 * n + 256]) * scale for n in range(3)]
    none = jnp.zeros((124, COLS), F32)
    keys = jnp.concatenate([k, none], axis=0).astype(BF)
    values = jnp.concatenate([v, none], axis=0).astype(BF)
    step = lax.broadcasted_iota(jnp.int32, (32, 128), 0)
    other = lax.broadcasted_iota(jnp.int32, (32, 128), 1)
    _, weight, accum = attend(q.astype(BF).astype(F32), keys, values, other * 8 <= step)
    heads = own_head(accum / weight)
    local[7].wait()
    r3[tp] = pack8(jnp.dot(pad8(heads).astype(BF), so_v[...], preferred_element_type=F32)[:4])
    spread(r3, tp, tp_peers, 3)

    a_from_y(1, 1)
    w_from_z(2)
    a_from_z(2)
    a_to_z(3)

    collect(r3, 8, 3)
    state1 = state0 + unpack8(jnp.sum(r3[...], axis=0))
    a, ss = scaled(state1, g_cross)
    local[8].wait()
    part = jnp.dot(a, cq_v[...], preferred_element_type=F32)[:4]
    part = jnp.concatenate([pack8(part), jnp.broadcast_to(pad8(ss), (8, 128))], axis=1)
    merge_pas(part, r4, r4z, 4)

    w_from_x(2, PASSED)
    w_from_x(3, KEPT)
    a_from_y(1, 2)
    merge_pas_z(r4, r4z, 4)
    a_from_z(3)
    w_from_x(2, KEPT)
    a_from_y(1, 3)

    for half in range(2):
        wait_bytes(a_all.at[:, pl.ds(0, 2 * COLS)], an_r.at[half])
    wait_bytes(w_all.at[0, pl.ds(0, 15 * OWN)], ws_r.at[0])
    for c in range(2):

        def tile(n, carry):
            cols = pl.ds(pl.multiple_of(n * 256, 256), 256)
            kv[c, :, cols] = jnp.dot(
                a_all[...], w_all[c, :, cols], preferred_element_type=F32
            ).astype(BF)
            return carry

        lax.fori_loop(0, 2, tile, 0)
    outs = [
        pltpu.make_async_copy(kv.at[0], kout, osem.at[0]),
        pltpu.make_async_copy(kv.at[1], vout, osem.at[1]),
    ]
    for c in outs:
        c.start()

    total = merged(r4z, 4)
    cquery = unpack8(total[:, :256]) * rms(total[:4, 256:257])

    slot = lax.broadcasted_iota(jnp.int32, (32, ROWS), 1)
    live = (slot < lens[0]) | ((slot >= PLEN) & (slot < lens[1] + PLEN))
    peak, weight, accum = attend(cquery.astype(BF).astype(F32), kv[0], kv[1], live)
    head = lax.broadcasted_iota(jnp.int32, (8, 128), 0)
    lane = lax.broadcasted_iota(jnp.int32, (8, 128), 1)
    rows = []
    for g in range(2):
        for s in range(STEPS):
            both = jnp.where(lane == head - 4 * g, peak[8 * s : 8 * s + 8], 0.0) + jnp.where(
                (lane >= 64) & (lane - 64 == head - 4 * g), weight[8 * s : 8 * s + 8], 0.0
            )
            rows.append(jnp.sum(both, axis=0, keepdims=True))
    r5[pas] = jnp.concatenate([pack8(own_head(accum)), jnp.concatenate(rows, axis=0)], axis=1)
    spread(r5, pas, pas_peers, 5)
    collect(r5, 16, 5)
    peaks = [r5[i, :, 256:384] for i in range(16)]
    top = peaks[0]
    for i in range(1, 16):
        top = jnp.maximum(top, peaks[i])
    shares = []
    weight = jnp.zeros((8, 128), F32)
    for i in range(16):
        share = jnp.where(lane < 4, jnp.exp(peaks[i] - top), 0.0)
        weight = weight + share * pltpu.roll(peaks[i], 64, 1)
        shares.append(share)
    inv = 1.0 / jnp.where(lane < 4, weight, 1.0)
    shares = jnp.concatenate([s * inv for s in shares], axis=0)
    lane_of = lax.broadcasted_iota(jnp.int32, (128, 256), 0)
    column = lax.broadcasted_iota(jnp.int32, (128, 256), 1)
    widen = jnp.where((column >= lane_of * DH) & (column < lane_of * DH + DH), 1.0, 0.0)
    wide = jnp.dot(
        shares, widen.astype(F32), preferred_element_type=F32, precision=lax.Precision.HIGHEST
    )
    mixed = jnp.zeros((8, 256), F32)
    for i in range(16):
        mixed = mixed + wide[8 * i : 8 * i + 8] * r5[i, :, :256]
    local[9].wait()
    heads = pad8(unpack8(mixed)).astype(BF)
    r6[tp] = pack8(jnp.dot(heads, co_v[...], preferred_element_type=F32)[:4])
    spread(r6, tp, tp_peers, 6)
    collect(r6, 8, 6)
    state2 = state1 + unpack8(jnp.sum(r6[...], axis=0))

    a, ss = scaled(state2, g_ffn)
    local[10].wait()
    local[11].wait()
    gated = jnp.dot(a, gate_v[...], preferred_element_type=F32)[:4]
    upper = jnp.dot(a, up_v[...], preferred_element_type=F32)[:4]
    r7[pas] = jnp.concatenate(
        [pack16(jnp.concatenate([gated, upper], axis=1)), split_sum(ss)], axis=1
    ).astype(BF)
    spread(r7, pas, pas_peers, 7)
    collect(r7, 16, 7)
    total = r7[0].astype(F32)
    for i in range(1, 16):
        total = total + r7[i].astype(F32)
    scale = rms(total[0:4, 640:641] + total[4:8, 640:641])
    scale = jnp.concatenate([scale, scale], axis=0)
    gated = total[0:8, :640] * scale
    upper = total[8:16, :640] * scale
    gelu = 0.5 * gated * (1.0 + jnp.tanh(0.7978845608028654 * (gated + 0.044715 * gated * gated * gated)))
    hidden = (gelu * upper).astype(BF)
    local[12].wait()
    low = jnp.dot(hidden, down_v[0:640], preferred_element_type=F32)
    high = jnp.dot(hidden, down_v[640:1280], preferred_element_type=F32)
    r8[tp] = pack8(low[:4] + high[4:8])
    spread(r8, tp, tp_peers, 8)
    collect(r8, 8, 8)
    whole = state2 + unpack8(jnp.sum(r8[...], axis=0))
    own = whole[:, 0:32]
    for t in range(1, 8):
        own = jnp.where(tp == t, whole[:, 32 * t : 32 * t + 32], own)
    out[...] = own

    for n, buf, count in (
        (0, r1a, 16),
        (1, r1b, 8),
        (2, r2, 4),
        (9, r2z, 4),
        (3, r3, 8),
        (4, r4, 4),
        (11, r4z, 4),
        (5, r5, 16),
        (6, r6, 8),
        (7, r7, 16),
        (8, r8, 8),
    ):
        wait_bytes(buf.at[pl.ds(0, count - 1)], es.at[n])
    wait_bytes(a_all.at[:, pl.ds(0, 7 * COLS)], big_s.at[0])
    wait_bytes(w_all.at[0, pl.ds(0, 15 * OWN)], big_s.at[1])
    wait_bytes(w_all.at[0, pl.ds(0, 15 * OWN)], big_s.at[2])
    for c in outs:
        c.wait()


def finish(out_a, k_a, v_a, out_b, k_b, v_b):
    out_b[...] = out_a[...]
    k_b[...] = k_a[...]
    v_b[...] = v_a[...]


def shards(
    token_ids,
    embedding,
    passages,
    passage_lengths,
    w_key,
    w_value,
    norm_self,
    w_self_query,
    w_self_key,
    w_self_value,
    w_self_out,
    norm_cross,
    w_cross_query,
    w_cross_out,
    norm_ffn,
    w_gate,
    w_up,
    w_down,
):
    smem = pl.BlockSpec(memory_space=pltpu.SMEM)
    vmem = pl.BlockSpec(memory_space=pltpu.VMEM)
    hbm = pl.BlockSpec(memory_space=pltpu.HBM)
    dma = pltpu.SemaphoreType.DMA
    results = pl.pallas_call(
        kernel,
        name="decoder_layer",
        out_shape=(
            jax.ShapeDtypeStruct((STEPS, 32), F32),
            jax.ShapeDtypeStruct((ROWS, COLS), BF),
            jax.ShapeDtypeStruct((ROWS, COLS), BF),
        ),
        in_specs=[smem, smem, vmem, vmem, vmem] + [hbm] * 13,
        out_specs=(vmem, hbm, hbm),
        scratch_shapes=[
            pltpu.VMEM((ROWS, D), BF),
            pltpu.VMEM((2, D, COLS), BF),
            pltpu.VMEM((2, ROWS, COLS), BF),
            pltpu.VMEM((VROWS, D), BF),
            pltpu.VMEM((OWN, COLS), BF),
            pltpu.VMEM((OWN, COLS), BF),
            pltpu.VMEM((OWN, COLS), BF),
            pltpu.VMEM((COLS, OWN), BF),
            pltpu.VMEM((OWN, COLS), BF),
            pltpu.VMEM((COLS, OWN), BF),
            pltpu.VMEM((OWN, FFC), BF),
            pltpu.VMEM((OWN, FFC), BF),
            pltpu.VMEM((FFC, OWN), BF),
            pltpu.VMEM((16, 8, 128), F32),
            pltpu.VMEM((16, 8, 128), F32),
            pltpu.VMEM((8, 8, 128), F32),
            pltpu.VMEM((4, 8, 896), F32),
            pltpu.VMEM((4, 8, 896), F32),
            pltpu.VMEM((8, 8, 128), F32),
            pltpu.VMEM((4, 8, 384), F32),
            pltpu.VMEM((4, 8, 384), F32),
            pltpu.VMEM((16, 8, 384), F32),
            pltpu.VMEM((8, 8, 128), F32),
            pltpu.VMEM((16, 16, 768), BF),
            pltpu.VMEM((8, 8, 128), F32),
            dma((13,)),
            dma((2,)),
            dma((ACH,)),
            dma((2, ACH)),
            dma((2,)),
            dma((3, WCH)),
            dma((3, 4, WCH)),
            dma((1,)),
            dma((3,)),
            dma((12,)),
            dma((12,)),
        ],
        compiler_params=pltpu.CompilerParams(
            collective_id=1, has_side_effects=True, vmem_limit_bytes=56 << 20
        ),
        cost_estimate=pl.CostEstimate(
            flops=2 * 2 * ROWS * COLS * D, bytes_accessed=16 << 20, transcendentals=1 << 20
        ),
    )(
        token_ids,
        passage_lengths,
        norm_self.reshape(32, 128),
        norm_cross.reshape(32, 128),
        norm_ffn.reshape(32, 128),
        passages,
        w_key,
        w_value,
        w_self_query,
        w_self_key,
        w_self_value,
        w_self_out,
        w_cross_query,
        w_cross_out,
        w_gate,
        w_up,
        w_down,
        embedding,
    )
    return pl.pallas_call(
        finish,
        name="finish",
        out_shape=tuple(jax.ShapeDtypeStruct(r.shape, r.dtype) for r in results),
        in_specs=[vmem] * 3,
        out_specs=(vmem, vmem, vmem),
        compiler_params=pltpu.CompilerParams(vmem_limit_bytes=56 << 20),
    )(*results)


def solution(mesh):
    in_specs = (
        P("pb"),
        P(("pas", "tp"), None),
        P(("pb", "pas"), "tp"),
        P(("pb", "pas")),
        P("pas", "tp"),
        P("pas", "tp"),
        P(),
        P("pas", "tp"),
        P("pas", "tp"),
        P("pas", "tp"),
        P("tp", "pas"),
        P(),
        P("pas", "tp"),
        P("tp", "pas"),
        P(),
        P("pas", "tp"),
        P("pas", "tp"),
        P("tp", "pas"),
    )
    out_specs = (P("pb", ("pas", "tp")), P(("pb", "pas"), "tp"), P(("pb", "pas"), "tp"))
    return jax.shard_map(shards, mesh=mesh, in_specs=in_specs, out_specs=out_specs, check_vma=False)
```

```python
import jax
import jax.numpy as jnp
from jax import lax
from jax.experimental import pallas as pl
from jax.experimental.pallas import tpu as pltpu
from jax.sharding import PartitionSpec as P

BF = jnp.bfloat16
F32 = jnp.float32
MESH = pl.DeviceIdType.MESH
D = 4096
DH = 64
PLEN = 256
STEPS = 4
ROWS = 512
COLS = 512
OWN = 256
FFC = 1280
VROWS = 251
ACH = 4
WCH = 2
ARO = ROWS // ACH
WRO = OWN // WCH
PASSED = ((1, 0), (3, 1))
KEPT = ((1, 1), (3, 0), (2, 0), (2, 1))
HALF = D // 2

SCHEDULE = (
    ("sz", 0), ("sy",), ("wp", 0), ("sz", 1), ("wz", 1), ("wz", 4), ("c1",),
    ("ay", 0, 0), ("ay", 0, 1), ("az", 0), ("sz", 2), ("wp", 1), ("wp", 4), ("wk", 0), ("c2",),
    ("ay", 0, 2), ("ay", 0, 3), ("wz", 2), ("wz", 5), ("c2z",),
    ("ay", 1, 0), ("az", 1), ("sz", 3), ("wp", 2), ("wp", 5), ("wk", 1), ("wk", 4), ("c3",),
    ("ay", 1, 1), ("wz", 3), ("wz", 6), ("az", 2), ("c4",),
    ("wp", 3), ("wp", 6), ("wk", 2), ("wk", 5), ("ay", 1, 2), ("c4z",),
    ("az", 3), ("wk", 3), ("wk", 6), ("ay", 1, 3), ("mm",), ("mm", 0), ("mm", 1), ("c5",),
)


def pack8(v):
    n = v.shape[1] // 2
    return jnp.concatenate([v[:, :n], v[:, n:]], axis=0)


def unpack8(p):
    return jnp.concatenate([p[:4], p[4:8]], axis=1)


def pack16(v):
    n = v.shape[1] // 4
    return jnp.concatenate([v[:, n * k : n * k + n] for k in range(4)], axis=0)


def unpack16(p):
    return jnp.concatenate([p[4 * k : 4 * k + 4] for k in range(4)], axis=1)


def pad8(v):
    return jnp.concatenate([v, jnp.zeros_like(v)], axis=0)


def head_mask():
    head = lax.broadcasted_iota(jnp.int32, (8, COLS), 0)
    lane = lax.broadcasted_iota(jnp.int32, (8, COLS), 1)
    return jnp.where((lane >= head * DH) & (lane < head * DH + DH), 1.0, 0.0).astype(F32)


def by_head(q):
    mask = head_mask()
    return jnp.concatenate([q[s : s + 1] * mask for s in range(STEPS)], axis=0).astype(BF)


def own_head(acc):
    mask = head_mask()
    rows = [
        jnp.sum(acc[8 * s : 8 * s + 8] * mask, axis=0, keepdims=True) for s in range(STEPS)
    ]
    return jnp.concatenate(rows, axis=0)


def attend(q, keys, values, live):
    scores = lax.dot_general(
        by_head(q), keys, (((1,), (1,)), ((), ())), preferred_element_type=F32
    ) * (1.0 / DH**0.5)
    scores = jnp.where(live, scores, -1e30)
    peak = jnp.max(scores, axis=1, keepdims=True)
    weights = jnp.where(live, jnp.exp(scores - peak), 0.0).astype(BF)
    total = jnp.sum(weights.astype(F32), axis=1, keepdims=True)
    accum = jnp.dot(weights, values, preferred_element_type=F32)
    return peak, total, accum


def split_sum(ss):
    hi = ss.astype(BF).astype(F32)
    lo = ss - hi
    z = jnp.zeros_like(ss)
    return jnp.broadcast_to(jnp.concatenate([hi, lo, z, z], axis=0), (16, 128))


def kernel(
    tok,
    lens,
    g_self,
    g_cross,
    g_ffn,
    passages,
    w_key,
    w_value,
    w_sq,
    w_sk,
    w_sv,
    w_so,
    w_cq,
    w_co,
    w_gate,
    w_up,
    w_down,
    emb,
    out,
    kout,
    vout,
    a_all,
    w_all,
    kv,
    sums,
    emb_v,
    sq_v,
    sk_v,
    sv_v,
    so_v,
    cq_v,
    co_v,
    gate_v,
    up_v,
    down_v,
    s1a,
    r1a,
    r1b,
    r2,
    r2z,
    r3,
    r4,
    r4z,
    r5,
    r6,
    r7,
    r8,
    lsem,
    osem,
    az_r,
    af_r,
    an_r,
    wz_r,
    wx_r,
    ws_r,
    big_s,
    es,
    er,
):
    pb = lax.axis_index("pb")
    pas = lax.axis_index("pas")
    tp = lax.axis_index("tp")
    x, zl = pas // 4, pas % 4
    zh, y = tp // 4, tp % 4
    xs = [(x + k) % 4 for k in range(4)]
    zs = [(zl + k) % 4 for k in range(4)]
    ys = [(y + k) % 4 for k in range(4)]
    xb = [(x - k + 4) % 4 for k in range(4)]
    zb = [(zl - k + 4) % 4 for k in range(4)]
    yb = [(y - k + 4) % 4 for k in range(4)]
    far = (2, 1, 3, 0)
    pas_peers = [
        (pb, xs[a] * 4 + zs[b], tp) for a in far for b in (3, 2, 1, 0) if (a, b) != (0, 0)
    ]
    tp_peers = [
        (pb, pas, (zh * 4 if b == 0 else (1 - zh) * 4) + ys[a])
        for b in (1, 0)
        for a in far
        if (a, b) != (0, 0)
    ]
    x_peers = {k: (pb, xs[k] * 4 + zl, tp) for k in (1, 3, 2)}
    z_peers = {k: (pb, x * 4 + zs[k], tp) for k in (1, 3, 2)}
    y_peers = {k: (pb, pas, zh * 4 + ys[k]) for k in (1, 3, 2)}
    z4_peer = (pb, pas, (1 - zh) * 4 + y)
    sibling = (1 - pb, pas, tp)

    pas0 = pl.multiple_of(pas * OWN, OWN)
    tp0 = pl.multiple_of(tp * COLS, COLS)
    loads = [
        (passages, a_all.at[:, pl.ds(tp0, COLS)]),
        (w_key, w_all.at[0, pl.ds(pas0, OWN)]),
        (w_value, w_all.at[1, pl.ds(pas0, OWN)]),
        (emb, emb_v),
        (w_sq, sq_v),
        (w_sk, sk_v),
        (w_sv, sv_v),
        (w_so, so_v),
        (w_cq, cq_v),
        (w_co, co_v),
        (w_gate, gate_v),
        (w_up, up_v),
        (w_down, down_v),
    ]
    local = [pltpu.make_async_copy(s, d, lsem.at[n]) for n, (s, d) in enumerate(loads)]
    for c in local:
        c.start()

    barrier = pltpu.get_barrier_semaphore()
    greet = pas_peers + tp_peers + [sibling]
    for d in greet:
        pl.semaphore_signal(barrier, inc=1, device_id=d, device_id_type=MESH)

    def send(src, dst, ssem, rsem, dev):
        pltpu.make_async_remote_copy(
            src_ref=src,
            dst_ref=dst,
            send_sem=ssem,
            recv_sem=rsem,
            device_id=dev,
            device_id_type=MESH,
        ).start()

    def wait_bytes(ref, sem):
        pltpu.make_async_copy(ref, ref, sem).wait()

    def a_piece(block, c):
        cols = pl.ds(pl.multiple_of(block * COLS, COLS), COLS)
        return a_all.at[pl.ds(c * ARO, ARO), cols]

    def w_piece(block, c):
        return w_all.at[pb, pl.ds(pl.multiple_of(block * OWN + c * WRO, WRO), WRO)]

    def a_to_z(c):
        piece = a_piece(tp, c)
        send(piece, piece, big_s.at[0], az_r.at[c], z4_peer)

    def a_to_y(half, block, c):
        piece = a_piece(block, c)
        for k, passed_on in ((1, c % 2 == 0), (3, c % 2 == 1)):
            rsem = af_r.at[half, c] if passed_on else an_r.at[half, c]
            send(piece, piece, big_s.at[0], rsem, y_peers[k])

    def a_from_z(c):
        block = (1 - zh) * 4 + y
        wait_bytes(a_piece(block, c), az_r.at[c])
        a_to_y(1, block, c)

    def a_from_y(half, c):
        k = 1 if c % 2 == 0 else 3
        block = (zh if half == 0 else 1 - zh) * 4 + yb[k]
        piece = a_piece(block, c)
        wait_bytes(piece, af_r.at[half, c])
        send(piece, piece, big_s.at[0], an_r.at[half, c], y_peers[k])

    def w_sibling(block, c):
        piece = w_piece(block, c)
        send(piece, piece, big_s.at[2], ws_r.at[0], sibling)

    def w_to_x(block, e, c):
        piece = w_piece(block, c)
        for k in (1, 3):
            send(piece, piece, big_s.at[1], wx_r.at[k - 1, e, c], x_peers[k])

    def w_to_z(block, up, n, c):
        piece = w_piece(block, c)

        @pl.when(zl < 3 if up else zl > 0)
        def _():
            to = (pb, pas + 1, tp) if up else (pb, pas - 1, tp)
            send(piece, piece, big_s.at[3], wz_r.at[n if up else n + 3, c], to)

    def origin(e):
        if e == 0:
            return None, zl
        if e < 4:
            return zl >= e, zl - e
        return zl + (e - 3) < 4, zl + (e - 3)

    def guarded(e, body):
        here, bz = origin(e)
        if here is None:
            body(bz)
        else:
            pl.when(here)(lambda: body(bz))

    def w_from_z(e):
        def body(bz):
            block = x * 4 + bz
            for c in range(WCH):
                wait_bytes(w_piece(block, c), wz_r.at[e - 1, c])
                if e not in (3, 6):
                    w_to_z(block, e < 4, e if e < 4 else e - 3, c)
                w_to_x(block, e, c)
                w_sibling(block, c)

        guarded(e, body)

    def w_from_x(e, pieces):
        def body(bz):
            for kx, c in pieces:
                block = xb[kx] * 4 + bz
                piece = w_piece(block, c)
                wait_bytes(piece, wx_r.at[kx - 1, e, c])
                if (kx, c) in PASSED:
                    send(piece, piece, big_s.at[1], wx_r.at[1, e, c], x_peers[kx])
                w_sibling(block, c)

        guarded(e, body)

    def spread(buf, me, peers, n):
        slot = buf.at[me]
        for p in peers:
            send(slot, slot, es.at[n], er.at[n], p)

    def collect(buf, count, n):
        wait_bytes(buf.at[pl.ds(0, count - 1)], er.at[n])

    def merge_pas(part, bx, bz, n):
        bx[x] = part
        for k in (2, 1, 3):
            send(bx.at[x], bx.at[x], es.at[n], er.at[n], x_peers[k])

    def merge_pas_z(bx, bz, n):
        wait_bytes(bx.at[pl.ds(0, 3)], er.at[n])
        bz[zl] = bx[0] + bx[1] + bx[2] + bx[3]
        for k in (3, 2, 1):
            send(bz.at[zl], bz.at[zl], es.at[n + 7], er.at[n + 7], z_peers[k])

    def merged(bz, n):
        wait_bytes(bz.at[pl.ds(0, 3)], er.at[n + 7])
        return bz[0] + bz[1] + bz[2] + bz[3]

    def gain(g):
        return jnp.concatenate([g[pl.ds(2 * pas, 1), :], g[pl.ds(2 * pas + 1, 1), :]], axis=1)

    local[3].wait()
    row = lax.broadcasted_iota(jnp.int32, (8, VROWS), 0)
    place = lax.broadcasted_iota(jnp.int32, (8, VROWS), 1) + (pas * 8 + tp) * VROWS
    wanted = jnp.full((8, VROWS), -1, jnp.int32)
    for s in range(STEPS):
        wanted = jnp.where(row == s, tok[s], wanted)
    onehot = jnp.where(place == wanted, 1.0, 0.0).astype(BF)
    mine = jnp.dot(onehot, emb_v[...], preferred_element_type=F32)
    for i in range(16):
        s1a[i] = pack8(mine[:4, OWN * i : OWN * i + OWN])
    r1a[pas] = s1a[pas]
    pl.semaphore_wait(barrier, len(greet))
    for p in pas_peers:
        send(s1a.at[p[1]], r1a.at[pas], es.at[0], er.at[0], p)

    for n in range(3):
        local[n].wait()
    for c in range(WCH):
        w_to_z(pas, True, 0, c)
        w_to_z(pas, False, 0, c)
        w_to_x(pas, 0, c)

    st = {}

    def c1():
        collect(r1a, 16, 0)
        r1b[tp] = jnp.sum(r1a[...], axis=0)
        spread(r1b, tp, tp_peers, 1)

    def scaled(state, g):
        ss = jnp.sum(state * state, axis=1, keepdims=True)
        return pad8(state * gain(g)).astype(BF), ss

    def rms(ss):
        return lax.rsqrt(ss * (1.0 / D) + 1e-06)

    def c2():
        collect(r1b, 8, 1)
        st["state0"] = unpack8(jnp.sum(r1b[...], axis=0))
        a, ss = scaled(st["state0"], g_self)
        parts = []
        for n, w in ((4, sq_v), (5, sk_v), (6, sv_v)):
            local[n].wait()
            parts.append(pack8(jnp.dot(a, w[...], preferred_element_type=F32)[:4]))
        parts.append(jnp.broadcast_to(pad8(ss), (8, 128)))
        merge_pas(jnp.concatenate(parts, axis=1), r2, r2z, 2)

    def c2z():
        merge_pas_z(r2, r2z, 2)

    def c3():
        total = merged(r2z, 2)
        scale = rms(total[:4, 768:769])
        q, k, v = [unpack8(total[:, 256 * n : 256 * n + 256]) * scale for n in range(3)]
        none = jnp.zeros((124, COLS), F32)
        keys = jnp.concatenate([k, none], axis=0).astype(BF)
        values = jnp.concatenate([v, none], axis=0).astype(BF)
        step = lax.broadcasted_iota(jnp.int32, (32, 128), 0)
        other = lax.broadcasted_iota(jnp.int32, (32, 128), 1)
        _, weight, accum = attend(q.astype(BF).astype(F32), keys, values, other * 8 <= step)
        heads = own_head(accum / weight)
        local[7].wait()
        r3[tp] = pack8(jnp.dot(pad8(heads).astype(BF), so_v[...], preferred_element_type=F32)[:4])
        spread(r3, tp, tp_peers, 3)

    def c4():
        collect(r3, 8, 3)
        st["state1"] = st["state0"] + unpack8(jnp.sum(r3[...], axis=0))
        a, ss = scaled(st["state1"], g_cross)
        local[8].wait()
        part = jnp.dot(a, cq_v[...], preferred_element_type=F32)[:4]
        part = jnp.concatenate([pack8(part), jnp.broadcast_to(pad8(ss), (8, 128))], axis=1)
        merge_pas(part, r4, r4z, 4)

    def c4z():
        merge_pas_z(r4, r4z, 4)

    def c5():
        total = merged(r4z, 4)
        st["cquery"] = unpack8(total[:, :256]) * rms(total[:4, 256:257])

    near = pl.ds(pl.multiple_of(zh * HALF, HALF), HALF)
    distant = pl.ds(pl.multiple_of((1 - zh) * HALF, HALF), HALF)

    def a_whole(half, c):
        wait_bytes(a_all.at[pl.ds(0, ARO), pl.ds(0, 2 * COLS)], an_r.at[half, c])

    def mm(part=None):
        if part is None:
            for c in range(ACH):
                a_whole(0, c)
            wait_bytes(w_all.at[0, pl.ds(0, 15 * OWN)], ws_r.at[0])
            rows, n_rows, cols = pl.ds(0, ROWS), ROWS, near
        else:
            for c in (2 * part, 2 * part + 1):
                a_whole(1, c)
            rows, n_rows, cols = pl.ds(part * 256, 256), 256, distant
        for c in range(2):

            def tile(n, carry):
                to = pl.ds(pl.multiple_of(n * 256, 256), 256)
                new = jnp.dot(a_all[rows, cols], w_all[c, cols, to], preferred_element_type=F32)
                if part is None:
                    sums[c, rows, to] = new
                else:
                    kv[c, rows, to] = (sums[c, rows, to] + new).astype(BF)
                return carry

            lax.fori_loop(0, 2, tile, 0)

    def sy():
        for c in range(ACH):
            a_to_y(0, tp, c)

    events = {
        "sz": a_to_z,
        "sy": sy,
        "az": a_from_z,
        "ay": a_from_y,
        "wz": w_from_z,
        "wp": lambda e: w_from_x(e, PASSED),
        "wk": lambda e: w_from_x(e, KEPT),
        "c1": c1,
        "c2": c2,
        "c2z": c2z,
        "c3": c3,
        "c4": c4,
        "c4z": c4z,
        "c5": c5,
        "mm": mm,
    }
    for event in SCHEDULE:
        events[event[0]](*event[1:])
    state1, cquery = st["state1"], st["cquery"]
    outs = [
        pltpu.make_async_copy(kv.at[0], kout, osem.at[0]),
        pltpu.make_async_copy(kv.at[1], vout, osem.at[1]),
    ]
    for c in outs:
        c.start()

    slot = lax.broadcasted_iota(jnp.int32, (32, ROWS), 1)
    live = (slot < lens[0]) | ((slot >= PLEN) & (slot < lens[1] + PLEN))
    peak, weight, accum = attend(cquery.astype(BF).astype(F32), kv[0], kv[1], live)
    head = lax.broadcasted_iota(jnp.int32, (8, 128), 0)
    lane = lax.broadcasted_iota(jnp.int32, (8, 128), 1)
    rows = []
    for g in range(2):
        for s in range(STEPS):
            both = jnp.where(lane == head - 4 * g, peak[8 * s : 8 * s + 8], 0.0) + jnp.where(
                (lane >= 64) & (lane - 64 == head - 4 * g), weight[8 * s : 8 * s + 8], 0.0
            )
            rows.append(jnp.sum(both, axis=0, keepdims=True))
    r5[pas] = jnp.concatenate([pack8(own_head(accum)), jnp.concatenate(rows, axis=0)], axis=1)
    spread(r5, pas, pas_peers, 5)
    collect(r5, 16, 5)
    peaks = [r5[i, :, 256:384] for i in range(16)]
    top = peaks[0]
    for i in range(1, 16):
        top = jnp.maximum(top, peaks[i])
    shares = []
    weight = jnp.zeros((8, 128), F32)
    for i in range(16):
        share = jnp.where(lane < 4, jnp.exp(peaks[i] - top), 0.0)
        weight = weight + share * pltpu.roll(peaks[i], 64, 1)
        shares.append(share)
    inv = 1.0 / jnp.where(lane < 4, weight, 1.0)
    shares = jnp.concatenate([s * inv for s in shares], axis=0)
    lane_of = lax.broadcasted_iota(jnp.int32, (128, 256), 0)
    column = lax.broadcasted_iota(jnp.int32, (128, 256), 1)
    widen = jnp.where((column >= lane_of * DH) & (column < lane_of * DH + DH), 1.0, 0.0)
    wide = jnp.dot(
        shares, widen.astype(F32), preferred_element_type=F32, precision=lax.Precision.HIGHEST
    )
    mixed = jnp.zeros((8, 256), F32)
    for i in range(16):
        mixed = mixed + wide[8 * i : 8 * i + 8] * r5[i, :, :256]
    local[9].wait()
    heads = pad8(unpack8(mixed)).astype(BF)
    r6[tp] = pack8(jnp.dot(heads, co_v[...], preferred_element_type=F32)[:4])
    spread(r6, tp, tp_peers, 6)
    collect(r6, 8, 6)
    state2 = state1 + unpack8(jnp.sum(r6[...], axis=0))

    a, ss = scaled(state2, g_ffn)
    local[10].wait()
    local[11].wait()
    gated = jnp.dot(a, gate_v[...], preferred_element_type=F32)[:4]
    upper = jnp.dot(a, up_v[...], preferred_element_type=F32)[:4]
    r7[pas] = jnp.concatenate(
        [pack16(jnp.concatenate([gated, upper], axis=1)), split_sum(ss)], axis=1
    ).astype(BF)
    spread(r7, pas, pas_peers, 7)
    collect(r7, 16, 7)
    total = r7[0].astype(F32)
    for i in range(1, 16):
        total = total + r7[i].astype(F32)
    scale = rms(total[0:4, 640:641] + total[4:8, 640:641])
    scale = jnp.concatenate([scale, scale], axis=0)
    gated = total[0:8, :640] * scale
    upper = total[8:16, :640] * scale
    gelu = 0.5 * gated * (1.0 + jnp.tanh(0.7978845608028654 * (gated + 0.044715 * gated * gated * gated)))
    hidden = (gelu * upper).astype(BF)
    local[12].wait()
    low = jnp.dot(hidden, down_v[0:640], preferred_element_type=F32)
    high = jnp.dot(hidden, down_v[640:1280], preferred_element_type=F32)
    r8[tp] = pack8(low[:4] + high[4:8])
    spread(r8, tp, tp_peers, 8)
    collect(r8, 8, 8)
    whole = state2 + unpack8(jnp.sum(r8[...], axis=0))
    own = whole[:, 0:32]
    for t in range(1, 8):
        own = jnp.where(tp == t, whole[:, 32 * t : 32 * t + 32], own)
    out[...] = own

    for n, buf, count in (
        (0, r1a, 16),
        (1, r1b, 8),
        (2, r2, 4),
        (9, r2z, 4),
        (3, r3, 8),
        (4, r4, 4),
        (11, r4z, 4),
        (5, r5, 16),
        (6, r6, 8),
        (7, r7, 16),
        (8, r8, 8),
    ):
        wait_bytes(buf.at[pl.ds(0, count - 1)], es.at[n])
    wait_bytes(a_all.at[:, pl.ds(0, 7 * COLS)], big_s.at[0])
    wait_bytes(w_all.at[0, pl.ds(0, 12 * OWN)], big_s.at[1])
    wait_bytes(w_all.at[0, pl.ds(0, OWN)], big_s.at[3])

    @pl.when((zl > 0) & (zl < 3))
    def _():
        wait_bytes(w_all.at[0, pl.ds(0, 4 * OWN)], big_s.at[3])

    wait_bytes(w_all.at[0, pl.ds(0, 15 * OWN)], big_s.at[2])
    for c in outs:
        c.wait()


def finish(out_a, k_a, v_a, out_b, k_b, v_b):
    out_b[...] = out_a[...]
    k_b[...] = k_a[...]
    v_b[...] = v_a[...]


def shards(
    token_ids,
    embedding,
    passages,
    passage_lengths,
    w_key,
    w_value,
    norm_self,
    w_self_query,
    w_self_key,
    w_self_value,
    w_self_out,
    norm_cross,
    w_cross_query,
    w_cross_out,
    norm_ffn,
    w_gate,
    w_up,
    w_down,
):
    smem = pl.BlockSpec(memory_space=pltpu.SMEM)
    vmem = pl.BlockSpec(memory_space=pltpu.VMEM)
    hbm = pl.BlockSpec(memory_space=pltpu.HBM)
    dma = pltpu.SemaphoreType.DMA
    results = pl.pallas_call(
        kernel,
        name="decoder_layer",
        out_shape=(
            jax.ShapeDtypeStruct((STEPS, 32), F32),
            jax.ShapeDtypeStruct((ROWS, COLS), BF),
            jax.ShapeDtypeStruct((ROWS, COLS), BF),
        ),
        in_specs=[smem, smem, vmem, vmem, vmem] + [hbm] * 13,
        out_specs=(vmem, hbm, hbm),
        scratch_shapes=[
            pltpu.VMEM((ROWS, D), BF),
            pltpu.VMEM((2, D, COLS), BF),
            pltpu.VMEM((2, ROWS, COLS), BF),
            pltpu.VMEM((2, ROWS, COLS), F32),
            pltpu.VMEM((VROWS, D), BF),
            pltpu.VMEM((OWN, COLS), BF),
            pltpu.VMEM((OWN, COLS), BF),
            pltpu.VMEM((OWN, COLS), BF),
            pltpu.VMEM((COLS, OWN), BF),
            pltpu.VMEM((OWN, COLS), BF),
            pltpu.VMEM((COLS, OWN), BF),
            pltpu.VMEM((OWN, FFC), BF),
            pltpu.VMEM((OWN, FFC), BF),
            pltpu.VMEM((FFC, OWN), BF),
            pltpu.VMEM((16, 8, 128), F32),
            pltpu.VMEM((16, 8, 128), F32),
            pltpu.VMEM((8, 8, 128), F32),
            pltpu.VMEM((4, 8, 896), F32),
            pltpu.VMEM((4, 8, 896), F32),
            pltpu.VMEM((8, 8, 128), F32),
            pltpu.VMEM((4, 8, 384), F32),
            pltpu.VMEM((4, 8, 384), F32),
            pltpu.VMEM((16, 8, 384), F32),
            pltpu.VMEM((8, 8, 128), F32),
            pltpu.VMEM((16, 16, 768), BF),
            pltpu.VMEM((8, 8, 128), F32),
            dma((13,)),
            dma((2,)),
            dma((ACH,)),
            dma((2, ACH)),
            dma((2, ACH)),
            dma((6, WCH)),
            dma((3, 7, WCH)),
            dma((1,)),
            dma((4,)),
            dma((12,)),
            dma((12,)),
        ],
        compiler_params=pltpu.CompilerParams(
            collective_id=1, has_side_effects=True, vmem_limit_bytes=56 << 20
        ),
        cost_estimate=pl.CostEstimate(
            flops=2 * 2 * ROWS * COLS * D, bytes_accessed=16 << 20, transcendentals=1 << 20
        ),
    )(
        token_ids,
        passage_lengths,
        norm_self.reshape(32, 128),
        norm_cross.reshape(32, 128),
        norm_ffn.reshape(32, 128),
        passages,
        w_key,
        w_value,
        w_self_query,
        w_self_key,
        w_self_value,
        w_self_out,
        w_cross_query,
        w_cross_out,
        w_gate,
        w_up,
        w_down,
        embedding,
    )
    return pl.pallas_call(
        finish,
        name="finish",
        out_shape=tuple(jax.ShapeDtypeStruct(r.shape, r.dtype) for r in results),
        in_specs=[vmem] * 3,
        out_specs=(vmem, vmem, vmem),
        compiler_params=pltpu.CompilerParams(vmem_limit_bytes=56 << 20),
    )(*results)


def solution(mesh):
    in_specs = (
        P("pb"),
        P(("pas", "tp"), None),
        P(("pb", "pas"), "tp"),
        P(("pb", "pas")),
        P("pas", "tp"),
        P("pas", "tp"),
        P(),
        P("pas", "tp"),
        P("pas", "tp"),
        P("pas", "tp"),
        P("tp", "pas"),
        P(),
        P("pas", "tp"),
        P("tp", "pas"),
        P(),
        P("pas", "tp"),
        P("pas", "tp"),
        P("tp", "pas"),
    )
    out_specs = (P("pb", ("pas", "tp")), P(("pb", "pas"), "tp"), P(("pb", "pas"), "tp"))
    return jax.shard_map(shards, mesh=mesh, in_specs=in_specs, out_specs=out_specs, check_vma=False)
```

```python
import jax
import jax.numpy as jnp
from jax import lax
from jax.experimental import pallas as pl
from jax.experimental.pallas import tpu as pltpu
from jax.sharding import PartitionSpec as P

BF = jnp.bfloat16
F32 = jnp.float32
MESH = pl.DeviceIdType.MESH
D = 4096
DH = 64
PLEN = 256
STEPS = 4
ROWS = 512
COLS = 512
OWN = 256
FFC = 1280
VROWS = 251
AROW = (0, 128, 256, 384, 512)
ACH = len(AROW) - 1
STRAIGHT = ((1, 3),)
WCH = 2
WRO = OWN // WCH
PASSED = tuple((1 if c % 2 == 0 else 3, c) for c in range(WCH))
KEPT = tuple((3 if c % 2 == 0 else 1, c) for c in range(WCH)) + tuple((2, c) for c in range(WCH))
HALF = D // 2

SCHEDULE = (
    ("sw",), ("sz", 0), ("sy",), ("wp", 0), ("wz", 1), ("wz", 4), ("sz", 1), ("ay", 0, 0), ("ay", 0, 1),
    ("c1",), ("wp", 1), ("wp", 4), ("wz", 2), ("wz", 5), ("az", 0), ("sz", 2), ("ay", 0, 2), ("ay", 0, 3),
    ("wk", 0), ("wp", 2), ("wp", 5), ("c2",), ("wz", 3), ("c2z",), ("wz", 6), ("az", 1), ("sz", 3),
    ("ay", 1, 0), ("wp", 6), ("wk", 1), ("wk", 4), ("ay", 1, 1), ("wp", 3), ("c3",), ("az", 2), ("wk", 2),
    ("wk", 5), ("ay", 1, 2), ("c4",), ("az", 3), ("wk", 3), ("wk", 6), ("c4z",), ("mm",), ("ay", 1, 3),
    ("mm", 0), ("c5",), ("mm", 1),
)


def pack8(v):
    n = v.shape[1] // 2
    return jnp.concatenate([v[:, :n], v[:, n:]], axis=0)


def unpack8(p):
    return jnp.concatenate([p[:4], p[4:8]], axis=1)


def pack16(v):
    n = v.shape[1] // 4
    return jnp.concatenate([v[:, n * k : n * k + n] for k in range(4)], axis=0)


def unpack16(p):
    return jnp.concatenate([p[4 * k : 4 * k + 4] for k in range(4)], axis=1)


def pad8(v):
    return jnp.concatenate([v, jnp.zeros_like(v)], axis=0)


def head_mask():
    head = lax.broadcasted_iota(jnp.int32, (8, COLS), 0)
    lane = lax.broadcasted_iota(jnp.int32, (8, COLS), 1)
    return jnp.where((lane >= head * DH) & (lane < head * DH + DH), 1.0, 0.0).astype(F32)


def by_head(q):
    mask = head_mask()
    return jnp.concatenate([q[s : s + 1] * mask for s in range(STEPS)], axis=0).astype(BF)


def own_head(acc):
    mask = head_mask()
    rows = [
        jnp.sum(acc[8 * s : 8 * s + 8] * mask, axis=0, keepdims=True) for s in range(STEPS)
    ]
    return jnp.concatenate(rows, axis=0)


def attend(q, keys, values, live):
    scores = lax.dot_general(
        by_head(q), keys, (((1,), (1,)), ((), ())), preferred_element_type=F32
    ) * (1.0 / DH**0.5)
    scores = jnp.where(live, scores, -1e30)
    peak = jnp.max(scores, axis=1, keepdims=True)
    weights = jnp.where(live, jnp.exp(scores - peak), 0.0).astype(BF)
    total = jnp.sum(weights.astype(F32), axis=1, keepdims=True)
    accum = jnp.dot(weights, values, preferred_element_type=F32)
    return peak, total, accum


def split_sum(ss):
    hi = ss.astype(BF).astype(F32)
    lo = ss - hi
    z = jnp.zeros_like(ss)
    return jnp.broadcast_to(jnp.concatenate([hi, lo, z, z], axis=0), (16, 128))


def kernel(
    tok,
    lens,
    g_self,
    g_cross,
    g_ffn,
    passages,
    w_key,
    w_value,
    w_sq,
    w_sk,
    w_sv,
    w_so,
    w_cq,
    w_co,
    w_gate,
    w_up,
    w_down,
    emb,
    out,
    kout,
    vout,
    a_all,
    w_all,
    kv,
    sums,
    emb_v,
    sq_v,
    sk_v,
    sv_v,
    so_v,
    cq_v,
    co_v,
    gate_v,
    up_v,
    down_v,
    s1a,
    r1a,
    r1b,
    r2,
    r2z,
    r3,
    r4,
    r4z,
    r5,
    r6,
    r7,
    r8,
    lsem,
    osem,
    az_r,
    af_r,
    an_r,
    wz_r,
    wx_r,
    ws_r,
    big_s,
    es,
    er,
):
    pb = lax.axis_index("pb")
    pas = lax.axis_index("pas")
    tp = lax.axis_index("tp")
    x, zl = pas // 4, pas % 4
    zh, y = tp // 4, tp % 4
    xs = [(x + k) % 4 for k in range(4)]
    zs = [(zl + k) % 4 for k in range(4)]
    ys = [(y + k) % 4 for k in range(4)]
    xb = [(x - k + 4) % 4 for k in range(4)]
    zb = [(zl - k + 4) % 4 for k in range(4)]
    yb = [(y - k + 4) % 4 for k in range(4)]
    far = (2, 1, 3, 0)
    pas_peers = [
        (pb, xs[a] * 4 + zs[b], tp) for a in far for b in (3, 2, 1, 0) if (a, b) != (0, 0)
    ]
    tp_peers = [
        (pb, pas, (zh * 4 if b == 0 else (1 - zh) * 4) + ys[a])
        for b in (1, 0)
        for a in far
        if (a, b) != (0, 0)
    ]
    x_peers = {k: (pb, xs[k] * 4 + zl, tp) for k in (1, 3, 2)}
    z_peers = {k: (pb, x * 4 + zs[k], tp) for k in (1, 3, 2)}
    y_peers = {k: (pb, pas, zh * 4 + ys[k]) for k in (1, 3, 2)}
    z4_peer = (pb, pas, (1 - zh) * 4 + y)
    sibling = (1 - pb, pas, tp)

    pas0 = pl.multiple_of(pas * OWN, OWN)
    tp0 = pl.multiple_of(tp * COLS, COLS)
    loads = [
        (passages, a_all.at[:, pl.ds(tp0, COLS)]),
        (w_key, w_all.at[0, pl.ds(pas0, OWN)]),
        (w_value, w_all.at[1, pl.ds(pas0, OWN)]),
        (emb, emb_v),
        (w_sq, sq_v),
        (w_sk, sk_v),
        (w_sv, sv_v),
        (w_so, so_v),
        (w_cq, cq_v),
        (w_co, co_v),
        (w_gate, gate_v),
        (w_up, up_v),
        (w_down, down_v),
    ]
    local = [pltpu.make_async_copy(s, d, lsem.at[n]) for n, (s, d) in enumerate(loads)]
    for c in local:
        c.start()

    barrier = pltpu.get_barrier_semaphore()
    greet = pas_peers + tp_peers + [sibling]
    for d in greet:
        pl.semaphore_signal(barrier, inc=1, device_id=d, device_id_type=MESH)

    def send(src, dst, ssem, rsem, dev):
        pltpu.make_async_remote_copy(
            src_ref=src,
            dst_ref=dst,
            send_sem=ssem,
            recv_sem=rsem,
            device_id=dev,
            device_id_type=MESH,
        ).start()

    def wait_bytes(ref, sem):
        pltpu.make_async_copy(ref, ref, sem).wait()

    def a_piece(block, c):
        cols = pl.ds(pl.multiple_of(block * COLS, COLS), COLS)
        return a_all.at[pl.ds(AROW[c], AROW[c + 1] - AROW[c]), cols]

    def w_piece(block, c):
        return w_all.at[pb, pl.ds(pl.multiple_of(block * OWN + c * WRO, WRO), WRO)]

    def a_to_z(c):
        piece = a_piece(tp, c)
        send(piece, piece, big_s.at[0], az_r.at[c], z4_peer)

    def a_to_y(half, block, c):
        piece = a_piece(block, c)
        for k, passed_on in ((1, c % 2 == 0), (3, c % 2 == 1)):
            passed_on = passed_on and (half, c) not in STRAIGHT
            rsem = af_r.at[half, c] if passed_on else an_r.at[half, c]
            send(piece, piece, big_s.at[0], rsem, y_peers[k])
        if (half, c) in STRAIGHT:
            send(piece, piece, big_s.at[0], an_r.at[half, c], y_peers[2])

    def a_from_z(c):
        block = (1 - zh) * 4 + y
        wait_bytes(a_piece(block, c), az_r.at[c])
        a_to_y(1, block, c)

    def a_from_y(half, c):
        if (half, c) in STRAIGHT:
            return
        k = 1 if c % 2 == 0 else 3
        block = (zh if half == 0 else 1 - zh) * 4 + yb[k]
        piece = a_piece(block, c)
        wait_bytes(piece, af_r.at[half, c])
        send(piece, piece, big_s.at[0], an_r.at[half, c], y_peers[k])

    def w_sibling(block, c):
        piece = w_piece(block, c)
        send(piece, piece, big_s.at[2], ws_r.at[0], sibling)

    def w_to_x(block, e, c):
        piece = w_piece(block, c)
        for k in (1, 3):
            send(piece, piece, big_s.at[1], wx_r.at[k - 1, e, c], x_peers[k])

    def w_to_z(block, up, n, c):
        piece = w_piece(block, c)

        @pl.when(zl < 3 if up else zl > 0)
        def _():
            to = (pb, pas + 1, tp) if up else (pb, pas - 1, tp)
            send(piece, piece, big_s.at[3], wz_r.at[n if up else n + 3, c], to)

    def origin(e):
        if e == 0:
            return None, zl
        if e < 4:
            return zl >= e, zl - e
        return zl + (e - 3) < 4, zl + (e - 3)

    def guarded(e, body):
        here, bz = origin(e)
        if here is None:
            body(bz)
        else:
            pl.when(here)(lambda: body(bz))

    def w_from_z(e):
        def body(bz):
            block = x * 4 + bz
            for c in range(WCH):
                wait_bytes(w_piece(block, c), wz_r.at[e - 1, c])
                if e not in (3, 6):
                    w_to_z(block, e < 4, e if e < 4 else e - 3, c)
                w_to_x(block, e, c)
                w_sibling(block, c)

        guarded(e, body)

    def w_from_x(e, pieces):
        def body(bz):
            for kx, c in pieces:
                block = xb[kx] * 4 + bz
                piece = w_piece(block, c)
                wait_bytes(piece, wx_r.at[kx - 1, e, c])
                if (kx, c) in PASSED:
                    send(piece, piece, big_s.at[1], wx_r.at[1, e, c], x_peers[kx])
                w_sibling(block, c)

        guarded(e, body)

    def spread(buf, me, peers, n):
        slot = buf.at[me]
        for p in peers:
            send(slot, slot, es.at[n], er.at[n], p)

    def collect(buf, count, n):
        wait_bytes(buf.at[pl.ds(0, count - 1)], er.at[n])

    def merge_pas(part, bx, bz, n):
        bx[x] = part
        for k in (2, 1, 3):
            send(bx.at[x], bx.at[x], es.at[n], er.at[n], x_peers[k])

    def merge_pas_z(bx, bz, n):
        wait_bytes(bx.at[pl.ds(0, 3)], er.at[n])
        bz[zl] = bx[0] + bx[1] + bx[2] + bx[3]
        for k in (3, 2, 1):
            send(bz.at[zl], bz.at[zl], es.at[n + 7], er.at[n + 7], z_peers[k])

    def merged(bz, n):
        wait_bytes(bz.at[pl.ds(0, 3)], er.at[n + 7])
        return bz[0] + bz[1] + bz[2] + bz[3]

    def gain(g):
        return jnp.concatenate([g[pl.ds(2 * pas, 1), :], g[pl.ds(2 * pas + 1, 1), :]], axis=1)

    local[3].wait()
    row = lax.broadcasted_iota(jnp.int32, (8, VROWS), 0)
    place = lax.broadcasted_iota(jnp.int32, (8, VROWS), 1) + (pas * 8 + tp) * VROWS
    wanted = jnp.full((8, VROWS), -1, jnp.int32)
    for s in range(STEPS):
        wanted = jnp.where(row == s, tok[s], wanted)
    onehot = jnp.where(place == wanted, 1.0, 0.0).astype(BF)
    mine = jnp.dot(onehot, emb_v[...], preferred_element_type=F32)
    for i in range(16):
        s1a[i] = pack8(mine[:4, OWN * i : OWN * i + OWN])
    r1a[pas] = s1a[pas]
    pl.semaphore_wait(barrier, len(greet))
    for p in pas_peers:
        send(s1a.at[p[1]], r1a.at[pas], es.at[0], er.at[0], p)

    for n in range(3):
        local[n].wait()
    st = {}

    def c1():
        collect(r1a, 16, 0)
        r1b[tp] = jnp.sum(r1a[...], axis=0)
        spread(r1b, tp, tp_peers, 1)

    def scaled(state, g):
        ss = jnp.sum(state * state, axis=1, keepdims=True)
        return pad8(state * gain(g)).astype(BF), ss

    def rms(ss):
        return lax.rsqrt(ss * (1.0 / D) + 1e-06)

    def c2():
        collect(r1b, 8, 1)
        st["state0"] = unpack8(jnp.sum(r1b[...], axis=0))
        a, ss = scaled(st["state0"], g_self)
        parts = []
        for n, w in ((4, sq_v), (5, sk_v), (6, sv_v)):
            local[n].wait()
            parts.append(pack8(jnp.dot(a, w[...], preferred_element_type=F32)[:4]))
        parts.append(jnp.broadcast_to(pad8(ss), (8, 128)))
        merge_pas(jnp.concatenate(parts, axis=1), r2, r2z, 2)

    def c2z():
        merge_pas_z(r2, r2z, 2)

    def c3():
        total = merged(r2z, 2)
        scale = rms(total[:4, 768:769])
        q, k, v = [unpack8(total[:, 256 * n : 256 * n + 256]) * scale for n in range(3)]
        none = jnp.zeros((124, COLS), F32)
        keys = jnp.concatenate([k, none], axis=0).astype(BF)
        values = jnp.concatenate([v, none], axis=0).astype(BF)
        step = lax.broadcasted_iota(jnp.int32, (32, 128), 0)
        other = lax.broadcasted_iota(jnp.int32, (32, 128), 1)
        _, weight, accum = attend(q.astype(BF).astype(F32), keys, values, other * 8 <= step)
        heads = own_head(accum / weight)
        local[7].wait()
        r3[tp] = pack8(jnp.dot(pad8(heads).astype(BF), so_v[...], preferred_element_type=F32)[:4])
        spread(r3, tp, tp_peers, 3)

    def c4():
        collect(r3, 8, 3)
        st["state1"] = st["state0"] + unpack8(jnp.sum(r3[...], axis=0))
        a, ss = scaled(st["state1"], g_cross)
        local[8].wait()
        part = jnp.dot(a, cq_v[...], preferred_element_type=F32)[:4]
        part = jnp.concatenate([pack8(part), jnp.broadcast_to(pad8(ss), (8, 128))], axis=1)
        merge_pas(part, r4, r4z, 4)

    def c4z():
        merge_pas_z(r4, r4z, 4)

    def c5():
        total = merged(r4z, 4)
        st["cquery"] = unpack8(total[:, :256]) * rms(total[:4, 256:257])

    near = pl.ds(pl.multiple_of(zh * HALF, HALF), HALF)
    distant = pl.ds(pl.multiple_of((1 - zh) * HALF, HALF), HALF)

    def a_whole(half, c):
        blocks = 3 if (half, c) in STRAIGHT else 2
        n = AROW[c + 1] - AROW[c]
        wait_bytes(a_all.at[pl.ds(0, n), pl.ds(0, blocks * COLS)], an_r.at[half, c])

    def mm(part=None):
        if part is None:
            for c in range(ACH):
                a_whole(0, c)
            wait_bytes(w_all.at[0, pl.ds(0, 15 * OWN)], ws_r.at[0])
            rows, cols = pl.ds(0, ROWS), near
        else:
            for c in (2 * part, 2 * part + 1):
                a_whole(1, c)
            first, last = AROW[2 * part], AROW[2 * part + 2]
            rows, cols = pl.ds(first, last - first), distant
        for c in range(2):

            def tile(n, carry):
                to = pl.ds(pl.multiple_of(n * 256, 256), 256)
                new = jnp.dot(a_all[rows, cols], w_all[c, cols, to], preferred_element_type=F32)
                if part is None:
                    sums[c, rows, to] = new
                else:
                    kv[c, rows, to] = (sums[c, rows, to] + new).astype(BF)
                return carry

            lax.fori_loop(0, 2, tile, 0)

    def sw():
        for c in range(WCH):
            w_to_z(pas, True, 0, c)
            w_to_z(pas, False, 0, c)
            w_to_x(pas, 0, c)

    def sy():
        for c in range(ACH):
            a_to_y(0, tp, c)

    events = {
        "sz": a_to_z,
        "sw": sw,
        "sy": sy,
        "az": a_from_z,
        "ay": a_from_y,
        "wz": w_from_z,
        "wp": lambda e: w_from_x(e, PASSED),
        "wk": lambda e: w_from_x(e, KEPT),
        "c1": c1,
        "c2": c2,
        "c2z": c2z,
        "c3": c3,
        "c4": c4,
        "c4z": c4z,
        "c5": c5,
        "mm": mm,
    }
    for event in SCHEDULE:
        events[event[0]](*event[1:])
    state1, cquery = st["state1"], st["cquery"]
    outs = [
        pltpu.make_async_copy(kv.at[0], kout, osem.at[0]),
        pltpu.make_async_copy(kv.at[1], vout, osem.at[1]),
    ]
    for c in outs:
        c.start()

    slot = lax.broadcasted_iota(jnp.int32, (32, ROWS), 1)
    live = (slot < lens[0]) | ((slot >= PLEN) & (slot < lens[1] + PLEN))
    peak, weight, accum = attend(cquery.astype(BF).astype(F32), kv[0], kv[1], live)
    head = lax.broadcasted_iota(jnp.int32, (8, 128), 0)
    lane = lax.broadcasted_iota(jnp.int32, (8, 128), 1)
    rows = []
    for g in range(2):
        for s in range(STEPS):
            both = jnp.where(lane == head - 4 * g, peak[8 * s : 8 * s + 8], 0.0) + jnp.where(
                (lane >= 64) & (lane - 64 == head - 4 * g), weight[8 * s : 8 * s + 8], 0.0
            )
            rows.append(jnp.sum(both, axis=0, keepdims=True))
    r5[pas] = jnp.concatenate([pack8(own_head(accum)), jnp.concatenate(rows, axis=0)], axis=1)
    spread(r5, pas, pas_peers, 5)
    collect(r5, 16, 5)
    peaks = [r5[i, :, 256:384] for i in range(16)]
    top = peaks[0]
    for i in range(1, 16):
        top = jnp.maximum(top, peaks[i])
    shares = []
    weight = jnp.zeros((8, 128), F32)
    for i in range(16):
        share = jnp.where(lane < 4, jnp.exp(peaks[i] - top), 0.0)
        weight = weight + share * pltpu.roll(peaks[i], 64, 1)
        shares.append(share)
    inv = 1.0 / jnp.where(lane < 4, weight, 1.0)
    shares = jnp.concatenate([s * inv for s in shares], axis=0)
    lane_of = lax.broadcasted_iota(jnp.int32, (128, 256), 0)
    column = lax.broadcasted_iota(jnp.int32, (128, 256), 1)
    widen = jnp.where((column >= lane_of * DH) & (column < lane_of * DH + DH), 1.0, 0.0)
    wide = jnp.dot(
        shares, widen.astype(F32), preferred_element_type=F32, precision=lax.Precision.HIGHEST
    )
    mixed = jnp.zeros((8, 256), F32)
    for i in range(16):
        mixed = mixed + wide[8 * i : 8 * i + 8] * r5[i, :, :256]
    local[9].wait()
    heads = pad8(unpack8(mixed)).astype(BF)
    r6[tp] = pack8(jnp.dot(heads, co_v[...], preferred_element_type=F32)[:4])
    spread(r6, tp, tp_peers, 6)
    collect(r6, 8, 6)
    state2 = state1 + unpack8(jnp.sum(r6[...], axis=0))

    a, ss = scaled(state2, g_ffn)
    local[10].wait()
    local[11].wait()
    gated = jnp.dot(a, gate_v[...], preferred_element_type=F32)[:4]
    upper = jnp.dot(a, up_v[...], preferred_element_type=F32)[:4]
    r7[pas] = jnp.concatenate(
        [pack16(jnp.concatenate([gated, upper], axis=1)), split_sum(ss)], axis=1
    ).astype(BF)
    spread(r7, pas, pas_peers, 7)
    collect(r7, 16, 7)
    total = r7[0].astype(F32)
    for i in range(1, 16):
        total = total + r7[i].astype(F32)
    scale = rms(total[0:4, 640:641] + total[4:8, 640:641])
    scale = jnp.concatenate([scale, scale], axis=0)
    gated = total[0:8, :640] * scale
    upper = total[8:16, :640] * scale
    gelu = 0.5 * gated * (1.0 + jnp.tanh(0.7978845608028654 * (gated + 0.044715 * gated * gated * gated)))
    hidden = (gelu * upper).astype(BF)
    local[12].wait()
    low = jnp.dot(hidden, down_v[0:640], preferred_element_type=F32)
    high = jnp.dot(hidden, down_v[640:1280], preferred_element_type=F32)
    r8[tp] = pack8(low[:4] + high[4:8])
    spread(r8, tp, tp_peers, 8)
    collect(r8, 8, 8)
    whole = state2 + unpack8(jnp.sum(r8[...], axis=0))
    own = whole[:, 0:32]
    for t in range(1, 8):
        own = jnp.where(tp == t, whole[:, 32 * t : 32 * t + 32], own)
    out[...] = own

    for n, buf, count in (
        (0, r1a, 16),
        (1, r1b, 8),
        (2, r2, 4),
        (9, r2z, 4),
        (3, r3, 8),
        (4, r4, 4),
        (11, r4z, 4),
        (5, r5, 16),
        (6, r6, 8),
        (7, r7, 16),
        (8, r8, 8),
    ):
        wait_bytes(buf.at[pl.ds(0, count - 1)], es.at[n])
    wait_bytes(a_all.at[:, pl.ds(0, 7 * COLS)], big_s.at[0])
    wait_bytes(w_all.at[0, pl.ds(0, 12 * OWN)], big_s.at[1])
    wait_bytes(w_all.at[0, pl.ds(0, OWN)], big_s.at[3])

    @pl.when((zl > 0) & (zl < 3))
    def _():
        wait_bytes(w_all.at[0, pl.ds(0, 4 * OWN)], big_s.at[3])

    wait_bytes(w_all.at[0, pl.ds(0, 15 * OWN)], big_s.at[2])
    for c in outs:
        c.wait()


def finish(out_a, k_a, v_a, out_b, k_b, v_b):
    out_b[...] = out_a[...]
    k_b[...] = k_a[...]
    v_b[...] = v_a[...]


def shards(
    token_ids,
    embedding,
    passages,
    passage_lengths,
    w_key,
    w_value,
    norm_self,
    w_self_query,
    w_self_key,
    w_self_value,
    w_self_out,
    norm_cross,
    w_cross_query,
    w_cross_out,
    norm_ffn,
    w_gate,
    w_up,
    w_down,
):
    smem = pl.BlockSpec(memory_space=pltpu.SMEM)
    vmem = pl.BlockSpec(memory_space=pltpu.VMEM)
    hbm = pl.BlockSpec(memory_space=pltpu.HBM)
    dma = pltpu.SemaphoreType.DMA
    results = pl.pallas_call(
        kernel,
        name="decoder_layer",
        out_shape=(
            jax.ShapeDtypeStruct((STEPS, 32), F32),
            jax.ShapeDtypeStruct((ROWS, COLS), BF),
            jax.ShapeDtypeStruct((ROWS, COLS), BF),
        ),
        in_specs=[smem, smem, vmem, vmem, vmem] + [hbm] * 13,
        out_specs=(vmem, hbm, hbm),
        scratch_shapes=[
            pltpu.VMEM((ROWS, D), BF),
            pltpu.VMEM((2, D, COLS), BF),
            pltpu.VMEM((2, ROWS, COLS), BF),
            pltpu.VMEM((2, ROWS, COLS), F32),
            pltpu.VMEM((VROWS, D), BF),
            pltpu.VMEM((OWN, COLS), BF),
            pltpu.VMEM((OWN, COLS), BF),
            pltpu.VMEM((OWN, COLS), BF),
            pltpu.VMEM((COLS, OWN), BF),
            pltpu.VMEM((OWN, COLS), BF),
            pltpu.VMEM((COLS, OWN), BF),
            pltpu.VMEM((OWN, FFC), BF),
            pltpu.VMEM((OWN, FFC), BF),
            pltpu.VMEM((FFC, OWN), BF),
            pltpu.VMEM((16, 8, 128), F32),
            pltpu.VMEM((16, 8, 128), F32),
            pltpu.VMEM((8, 8, 128), F32),
            pltpu.VMEM((4, 8, 896), F32),
            pltpu.VMEM((4, 8, 896), F32),
            pltpu.VMEM((8, 8, 128), F32),
            pltpu.VMEM((4, 8, 384), F32),
            pltpu.VMEM((4, 8, 384), F32),
            pltpu.VMEM((16, 8, 384), F32),
            pltpu.VMEM((8, 8, 128), F32),
            pltpu.VMEM((16, 16, 768), BF),
            pltpu.VMEM((8, 8, 128), F32),
            dma((13,)),
            dma((2,)),
            dma((ACH,)),
            dma((2, ACH)),
            dma((2, ACH)),
            dma((6, WCH)),
            dma((3, 7, WCH)),
            dma((1,)),
            dma((4,)),
            dma((12,)),
            dma((12,)),
        ],
        compiler_params=pltpu.CompilerParams(
            collective_id=1, has_side_effects=True, vmem_limit_bytes=56 << 20
        ),
        cost_estimate=pl.CostEstimate(
            flops=2 * 2 * ROWS * COLS * D, bytes_accessed=16 << 20, transcendentals=1 << 20
        ),
    )(
        token_ids,
        passage_lengths,
        norm_self.reshape(32, 128),
        norm_cross.reshape(32, 128),
        norm_ffn.reshape(32, 128),
        passages,
        w_key,
        w_value,
        w_self_query,
        w_self_key,
        w_self_value,
        w_self_out,
        w_cross_query,
        w_cross_out,
        w_gate,
        w_up,
        w_down,
        embedding,
    )
    return pl.pallas_call(
        finish,
        name="finish",
        out_shape=tuple(jax.ShapeDtypeStruct(r.shape, r.dtype) for r in results),
        in_specs=[vmem] * 3,
        out_specs=(vmem, vmem, vmem),
        compiler_params=pltpu.CompilerParams(vmem_limit_bytes=56 << 20),
    )(*results)


def solution(mesh):
    in_specs = (
        P("pb"),
        P(("pas", "tp"), None),
        P(("pb", "pas"), "tp"),
        P(("pb", "pas")),
        P("pas", "tp"),
        P("pas", "tp"),
        P(),
        P("pas", "tp"),
        P("pas", "tp"),
        P("pas", "tp"),
        P("tp", "pas"),
        P(),
        P("pas", "tp"),
        P("tp", "pas"),
        P(),
        P("pas", "tp"),
        P("pas", "tp"),
        P("tp", "pas"),
    )
    out_specs = (P("pb", ("pas", "tp")), P(("pb", "pas"), "tp"), P(("pb", "pas"), "tp"))
    return jax.shard_map(shards, mesh=mesh, in_specs=in_specs, out_specs=out_specs, check_vma=False)
```

```python
import jax
import jax.numpy as jnp
from jax import lax
from jax.experimental import pallas as pl
from jax.experimental.pallas import tpu as pltpu
from jax.sharding import PartitionSpec as P

BF = jnp.bfloat16
F32 = jnp.float32
MESH = pl.DeviceIdType.MESH
D = 4096
DH = 64
PLEN = 256
STEPS = 4
ROWS = 512
COLS = 512
OWN = 256
FFC = 1280
VROWS = 251
AROW = (0, 128, 256, 384, 512)
ACH = len(AROW) - 1
STRAIGHT = ((1, 0), (1, 1), (1, 2), (1, 3))
WCH = 2
WRO = OWN // WCH
PASSED = tuple((1 if c % 2 == 0 else 3, c) for c in range(WCH))
KEPT = tuple((3 if c % 2 == 0 else 1, c) for c in range(WCH)) + tuple((2, c) for c in range(WCH))
HALF = D // 2

SCHEDULE = (
    ("sw",), ("sz", 0), ("sy", 0), ("sy", 1), ("sy", 2), ("sy", 3), ("e1",), ("wp", 0), ("wz", 1), ("wz", 4),
    ("sz", 1), ("ay", 0, 0), ("ay", 0, 1), ("c1",), ("wp", 1), ("wp", 4), ("wz", 2), ("wz", 5), ("az", 0),
    ("sz", 2), ("ay", 0, 2), ("ay", 0, 3), ("wk", 0), ("c2",), ("wp", 2), ("wp", 5), ("c2z",), ("wz", 3),
    ("wz", 6), ("az", 1), ("sz", 3), ("ay", 1, 0), ("wp", 6), ("wk", 1), ("wk", 4), ("ay", 1, 1), ("wp", 3),
    ("c3",), ("az", 2), ("wk", 2), ("wk", 5), ("ay", 1, 2), ("c4",), ("az", 3), ("wk", 3), ("wk", 6),
    ("c4z",), ("mm",), ("ay", 1, 3), ("mm", 0), ("c5",), ("mm", 1),
)


def pack8(v):
    n = v.shape[1] // 2
    return jnp.concatenate([v[:, :n], v[:, n:]], axis=0)


def unpack8(p):
    return jnp.concatenate([p[:4], p[4:8]], axis=1)


def pack16(v):
    n = v.shape[1] // 4
    return jnp.concatenate([v[:, n * k : n * k + n] for k in range(4)], axis=0)


def unpack16(p):
    return jnp.concatenate([p[4 * k : 4 * k + 4] for k in range(4)], axis=1)


def pad8(v):
    return jnp.concatenate([v, jnp.zeros_like(v)], axis=0)


def head_mask():
    head = lax.broadcasted_iota(jnp.int32, (8, COLS), 0)
    lane = lax.broadcasted_iota(jnp.int32, (8, COLS), 1)
    return jnp.where((lane >= head * DH) & (lane < head * DH + DH), 1.0, 0.0).astype(F32)


def by_head(q):
    mask = head_mask()
    return jnp.concatenate([q[s : s + 1] * mask for s in range(STEPS)], axis=0).astype(BF)


def own_head(acc):
    mask = head_mask()
    rows = [
        jnp.sum(acc[8 * s : 8 * s + 8] * mask, axis=0, keepdims=True) for s in range(STEPS)
    ]
    return jnp.concatenate(rows, axis=0)


def attend(q, keys, values, live):
    scores = lax.dot_general(
        by_head(q), keys, (((1,), (1,)), ((), ())), preferred_element_type=F32
    ) * (1.0 / DH**0.5)
    scores = jnp.where(live, scores, -1e30)
    peak = jnp.max(scores, axis=1, keepdims=True)
    weights = jnp.where(live, jnp.exp(scores - peak), 0.0).astype(BF)
    total = jnp.sum(weights.astype(F32), axis=1, keepdims=True)
    accum = jnp.dot(weights, values, preferred_element_type=F32)
    return peak, total, accum


def split_sum(ss):
    hi = ss.astype(BF).astype(F32)
    lo = ss - hi
    z = jnp.zeros_like(ss)
    return jnp.broadcast_to(jnp.concatenate([hi, lo, z, z], axis=0), (16, 128))


def kernel(
    tok,
    lens,
    g_self,
    g_cross,
    g_ffn,
    passages,
    w_key,
    w_value,
    w_sq,
    w_sk,
    w_sv,
    w_so,
    w_cq,
    w_co,
    w_gate,
    w_up,
    w_down,
    emb,
    out,
    kout,
    vout,
    a_all,
    w_all,
    kv,
    sums,
    emb_v,
    sq_v,
    sk_v,
    sv_v,
    so_v,
    cq_v,
    co_v,
    gate_v,
    up_v,
    down_v,
    s1a,
    r1a,
    r1b,
    r2,
    r2z,
    r3,
    r4,
    r4z,
    r5,
    r6,
    r7,
    r8,
    lsem,
    osem,
    az_r,
    af_r,
    an_r,
    wz_r,
    wx_r,
    ws_r,
    big_s,
    es,
    er,
):
    pb = lax.axis_index("pb")
    pas = lax.axis_index("pas")
    tp = lax.axis_index("tp")
    x, zl = pas // 4, pas % 4
    zh, y = tp // 4, tp % 4
    xs = [(x + k) % 4 for k in range(4)]
    zs = [(zl + k) % 4 for k in range(4)]
    ys = [(y + k) % 4 for k in range(4)]
    xb = [(x - k + 4) % 4 for k in range(4)]
    zb = [(zl - k + 4) % 4 for k in range(4)]
    yb = [(y - k + 4) % 4 for k in range(4)]
    far = (2, 1, 3, 0)
    pas_peers = [
        (pb, xs[a] * 4 + zs[b], tp) for a in far for b in (3, 2, 1, 0) if (a, b) != (0, 0)
    ]
    tp_peers = [
        (pb, pas, (zh * 4 if b == 0 else (1 - zh) * 4) + ys[a])
        for b in (1, 0)
        for a in far
        if (a, b) != (0, 0)
    ]
    x_peers = {k: (pb, xs[k] * 4 + zl, tp) for k in (1, 3, 2)}
    z_peers = {k: (pb, x * 4 + zs[k], tp) for k in (1, 3, 2)}
    y_peers = {k: (pb, pas, zh * 4 + ys[k]) for k in (1, 3, 2)}
    z4_peer = (pb, pas, (1 - zh) * 4 + y)
    sibling = (1 - pb, pas, tp)

    barrier = pltpu.get_barrier_semaphore()
    greet = pas_peers + tp_peers + [sibling]
    for d in greet:
        pl.semaphore_signal(barrier, inc=1, device_id=d, device_id_type=MESH)

    pas0 = pl.multiple_of(pas * OWN, OWN)
    tp0 = pl.multiple_of(tp * COLS, COLS)
    loads = [
        (passages, a_all.at[:, pl.ds(tp0, COLS)]),
        (w_key, w_all.at[0, pl.ds(pas0, OWN)]),
        (w_value, w_all.at[1, pl.ds(pas0, OWN)]),
        (emb, emb_v),
        (w_sq, sq_v),
        (w_sk, sk_v),
        (w_sv, sv_v),
        (w_so, so_v),
        (w_cq, cq_v),
        (w_co, co_v),
        (w_gate, gate_v),
        (w_up, up_v),
        (w_down, down_v),
    ]
    local = [pltpu.make_async_copy(s, d, lsem.at[n]) for n, (s, d) in enumerate(loads)]
    for c in local[:3]:
        c.start()

    def send(src, dst, ssem, rsem, dev):
        pltpu.make_async_remote_copy(
            src_ref=src,
            dst_ref=dst,
            send_sem=ssem,
            recv_sem=rsem,
            device_id=dev,
            device_id_type=MESH,
        ).start()

    def wait_bytes(ref, sem):
        pltpu.make_async_copy(ref, ref, sem).wait()

    def a_piece(block, c):
        cols = pl.ds(pl.multiple_of(block * COLS, COLS), COLS)
        return a_all.at[pl.ds(AROW[c], AROW[c + 1] - AROW[c]), cols]

    def w_piece(block, c):
        return w_all.at[pb, pl.ds(pl.multiple_of(block * OWN + c * WRO, WRO), WRO)]

    def a_to_z(c):
        piece = a_piece(tp, c)
        send(piece, piece, big_s.at[0], az_r.at[c], z4_peer)

    def a_to_y(half, block, c):
        piece = a_piece(block, c)
        for k, passed_on in ((1, c % 2 == 0), (3, c % 2 == 1)):
            passed_on = passed_on and (half, c) not in STRAIGHT
            rsem = af_r.at[half, c] if passed_on else an_r.at[half, c]
            send(piece, piece, big_s.at[0], rsem, y_peers[k])
        if (half, c) in STRAIGHT:
            send(piece, piece, big_s.at[0], an_r.at[half, c], y_peers[2])

    def a_from_z(c):
        block = (1 - zh) * 4 + y
        wait_bytes(a_piece(block, c), az_r.at[c])
        a_to_y(1, block, c)

    def a_from_y(half, c):
        if (half, c) in STRAIGHT:
            return
        k = 1 if c % 2 == 0 else 3
        block = (zh if half == 0 else 1 - zh) * 4 + yb[k]
        piece = a_piece(block, c)
        wait_bytes(piece, af_r.at[half, c])
        send(piece, piece, big_s.at[0], an_r.at[half, c], y_peers[k])

    def w_sibling(block, c):
        piece = w_piece(block, c)
        send(piece, piece, big_s.at[2], ws_r.at[0], sibling)

    def w_to_x(block, e, c):
        piece = w_piece(block, c)
        for k in (1, 3):
            send(piece, piece, big_s.at[1], wx_r.at[k - 1, e, c], x_peers[k])

    def w_to_z(block, up, n, c):
        piece = w_piece(block, c)

        @pl.when(zl < 3 if up else zl > 0)
        def _():
            to = (pb, pas + 1, tp) if up else (pb, pas - 1, tp)
            send(piece, piece, big_s.at[3], wz_r.at[n if up else n + 3, c], to)

    def origin(e):
        if e == 0:
            return None, zl
        if e < 4:
            return zl >= e, zl - e
        return zl + (e - 3) < 4, zl + (e - 3)

    def guarded(e, body):
        here, bz = origin(e)
        if here is None:
            body(bz)
        else:
            pl.when(here)(lambda: body(bz))

    def w_from_z(e):
        def body(bz):
            block = x * 4 + bz
            for c in range(WCH):
                wait_bytes(w_piece(block, c), wz_r.at[e - 1, c])
                if e not in (3, 6):
                    w_to_z(block, e < 4, e if e < 4 else e - 3, c)
                w_to_x(block, e, c)
                w_sibling(block, c)

        guarded(e, body)

    def w_from_x(e, pieces):
        def body(bz):
            for kx, c in pieces:
                block = xb[kx] * 4 + bz
                piece = w_piece(block, c)
                wait_bytes(piece, wx_r.at[kx - 1, e, c])
                if (kx, c) in PASSED:
                    send(piece, piece, big_s.at[1], wx_r.at[1, e, c], x_peers[kx])
                w_sibling(block, c)

        guarded(e, body)

    def spread(buf, me, peers, n):
        slot = buf.at[me]
        for p in peers:
            send(slot, slot, es.at[n], er.at[n], p)

    def collect(buf, count, n):
        wait_bytes(buf.at[pl.ds(0, count - 1)], er.at[n])

    def merge_pas(part, bx, bz, n):
        bx[x] = part
        for k in (2, 1, 3):
            send(bx.at[x], bx.at[x], es.at[n], er.at[n], x_peers[k])

    def merge_pas_z(bx, bz, n):
        wait_bytes(bx.at[pl.ds(0, 3)], er.at[n])
        bz[zl] = bx[0] + bx[1] + bx[2] + bx[3]
        for k in (3, 2, 1):
            send(bz.at[zl], bz.at[zl], es.at[n + 7], er.at[n + 7], z_peers[k])

    def merged(bz, n):
        wait_bytes(bz.at[pl.ds(0, 3)], er.at[n + 7])
        return bz[0] + bz[1] + bz[2] + bz[3]

    def gain(g):
        return jnp.concatenate([g[pl.ds(2 * pas, 1), :], g[pl.ds(2 * pas + 1, 1), :]], axis=1)

    pl.semaphore_wait(barrier, len(greet))
    for n in range(3):
        local[n].wait()
    for c in local[3:]:
        c.start()
    st = {}

    def e1():
        local[3].wait()
        row = lax.broadcasted_iota(jnp.int32, (8, VROWS), 0)
        place = lax.broadcasted_iota(jnp.int32, (8, VROWS), 1) + (pas * 8 + tp) * VROWS
        wanted = jnp.full((8, VROWS), -1, jnp.int32)
        for s in range(STEPS):
            wanted = jnp.where(row == s, tok[s], wanted)
        onehot = jnp.where(place == wanted, 1.0, 0.0).astype(BF)
        mine = jnp.dot(onehot, emb_v[...], preferred_element_type=F32)
        for i in range(16):
            s1a[i] = pack8(mine[:4, OWN * i : OWN * i + OWN])
        r1a[pas] = s1a[pas]
        for p in pas_peers:
            send(s1a.at[p[1]], r1a.at[pas], es.at[0], er.at[0], p)

    def c1():
        collect(r1a, 16, 0)
        r1b[tp] = jnp.sum(r1a[...], axis=0)
        spread(r1b, tp, tp_peers, 1)

    def scaled(state, g):
        ss = jnp.sum(state * state, axis=1, keepdims=True)
        return pad8(state * gain(g)).astype(BF), ss

    def rms(ss):
        return lax.rsqrt(ss * (1.0 / D) + 1e-06)

    def c2():
        collect(r1b, 8, 1)
        st["state0"] = unpack8(jnp.sum(r1b[...], axis=0))
        a, ss = scaled(st["state0"], g_self)
        parts = []
        for n, w in ((4, sq_v), (5, sk_v), (6, sv_v)):
            local[n].wait()
            parts.append(pack8(jnp.dot(a, w[...], preferred_element_type=F32)[:4]))
        parts.append(jnp.broadcast_to(pad8(ss), (8, 128)))
        merge_pas(jnp.concatenate(parts, axis=1), r2, r2z, 2)

    def c2z():
        merge_pas_z(r2, r2z, 2)

    def c3():
        total = merged(r2z, 2)
        scale = rms(total[:4, 768:769])
        q, k, v = [unpack8(total[:, 256 * n : 256 * n + 256]) * scale for n in range(3)]
        none = jnp.zeros((124, COLS), F32)
        keys = jnp.concatenate([k, none], axis=0).astype(BF)
        values = jnp.concatenate([v, none], axis=0).astype(BF)
        step = lax.broadcasted_iota(jnp.int32, (32, 128), 0)
        other = lax.broadcasted_iota(jnp.int32, (32, 128), 1)
        _, weight, accum = attend(q.astype(BF).astype(F32), keys, values, other * 8 <= step)
        heads = own_head(accum / weight)
        local[7].wait()
        r3[tp] = pack8(jnp.dot(pad8(heads).astype(BF), so_v[...], preferred_element_type=F32)[:4])
        spread(r3, tp, tp_peers, 3)

    def c4():
        collect(r3, 8, 3)
        st["state1"] = st["state0"] + unpack8(jnp.sum(r3[...], axis=0))
        a, ss = scaled(st["state1"], g_cross)
        local[8].wait()
        part = jnp.dot(a, cq_v[...], preferred_element_type=F32)[:4]
        part = jnp.concatenate([pack8(part), jnp.broadcast_to(pad8(ss), (8, 128))], axis=1)
        merge_pas(part, r4, r4z, 4)

    def c4z():
        merge_pas_z(r4, r4z, 4)

    def c5():
        total = merged(r4z, 4)
        st["cquery"] = unpack8(total[:, :256]) * rms(total[:4, 256:257])

    near = pl.ds(pl.multiple_of(zh * HALF, HALF), HALF)
    distant = pl.ds(pl.multiple_of((1 - zh) * HALF, HALF), HALF)

    def a_whole(half, c):
        blocks = 3 if (half, c) in STRAIGHT else 2
        n = AROW[c + 1] - AROW[c]
        wait_bytes(a_all.at[pl.ds(0, n), pl.ds(0, blocks * COLS)], an_r.at[half, c])

    def mm(part=None):
        if part is None:
            for c in range(ACH):
                a_whole(0, c)
            wait_bytes(w_all.at[0, pl.ds(0, 15 * OWN)], ws_r.at[0])
            rows, cols = pl.ds(0, ROWS), near
        else:
            for c in (2 * part, 2 * part + 1):
                a_whole(1, c)
            first, last = AROW[2 * part], AROW[2 * part + 2]
            rows, cols = pl.ds(first, last - first), distant
        for c in range(2):

            def tile(n, carry):
                to = pl.ds(pl.multiple_of(n * 256, 256), 256)
                new = jnp.dot(a_all[rows, cols], w_all[c, cols, to], preferred_element_type=F32)
                if part is None:
                    sums[c, rows, to] = new
                else:
                    kv[c, rows, to] = (sums[c, rows, to] + new).astype(BF)
                return carry

            lax.fori_loop(0, 2, tile, 0)

    def sw():
        for c in range(WCH):
            w_to_z(pas, True, 0, c)
            w_to_z(pas, False, 0, c)
            w_to_x(pas, 0, c)

    def sy(c):
        a_to_y(0, tp, c)

    events = {
        "sz": a_to_z,
        "sw": sw,
        "sy": sy,
        "az": a_from_z,
        "ay": a_from_y,
        "wz": w_from_z,
        "wp": lambda e: w_from_x(e, PASSED),
        "wk": lambda e: w_from_x(e, KEPT),
        "e1": e1,
        "c1": c1,
        "c2": c2,
        "c2z": c2z,
        "c3": c3,
        "c4": c4,
        "c4z": c4z,
        "c5": c5,
        "mm": mm,
    }
    for event in SCHEDULE:
        events[event[0]](*event[1:])
    state1, cquery = st["state1"], st["cquery"]
    outs = [
        pltpu.make_async_copy(kv.at[0], kout, osem.at[0]),
        pltpu.make_async_copy(kv.at[1], vout, osem.at[1]),
    ]
    for c in outs:
        c.start()

    slot = lax.broadcasted_iota(jnp.int32, (32, ROWS), 1)
    live = (slot < lens[0]) | ((slot >= PLEN) & (slot < lens[1] + PLEN))
    peak, weight, accum = attend(cquery.astype(BF).astype(F32), kv[0], kv[1], live)
    head = lax.broadcasted_iota(jnp.int32, (8, 128), 0)
    lane = lax.broadcasted_iota(jnp.int32, (8, 128), 1)
    rows = []
    for g in range(2):
        for s in range(STEPS):
            both = jnp.where(lane == head - 4 * g, peak[8 * s : 8 * s + 8], 0.0) + jnp.where(
                (lane >= 64) & (lane - 64 == head - 4 * g), weight[8 * s : 8 * s + 8], 0.0
            )
            rows.append(jnp.sum(both, axis=0, keepdims=True))
    r5[pas] = jnp.concatenate([pack8(own_head(accum)), jnp.concatenate(rows, axis=0)], axis=1)
    spread(r5, pas, pas_peers, 5)
    collect(r5, 16, 5)
    peaks = [r5[i, :, 256:384] for i in range(16)]
    top = peaks[0]
    for i in range(1, 16):
        top = jnp.maximum(top, peaks[i])
    shares = []
    weight = jnp.zeros((8, 128), F32)
    for i in range(16):
        share = jnp.where(lane < 4, jnp.exp(peaks[i] - top), 0.0)
        weight = weight + share * pltpu.roll(peaks[i], 64, 1)
        shares.append(share)
    inv = 1.0 / jnp.where(lane < 4, weight, 1.0)
    shares = jnp.concatenate([s * inv for s in shares], axis=0)
    lane_of = lax.broadcasted_iota(jnp.int32, (128, 256), 0)
    column = lax.broadcasted_iota(jnp.int32, (128, 256), 1)
    widen = jnp.where((column >= lane_of * DH) & (column < lane_of * DH + DH), 1.0, 0.0)
    wide = jnp.dot(
        shares, widen.astype(F32), preferred_element_type=F32, precision=lax.Precision.HIGHEST
    )
    mixed = jnp.zeros((8, 256), F32)
    for i in range(16):
        mixed = mixed + wide[8 * i : 8 * i + 8] * r5[i, :, :256]
    local[9].wait()
    heads = pad8(unpack8(mixed)).astype(BF)
    r6[tp] = pack8(jnp.dot(heads, co_v[...], preferred_element_type=F32)[:4])
    spread(r6, tp, tp_peers, 6)
    collect(r6, 8, 6)
    state2 = state1 + unpack8(jnp.sum(r6[...], axis=0))

    a, ss = scaled(state2, g_ffn)
    local[10].wait()
    local[11].wait()
    gated = jnp.dot(a, gate_v[...], preferred_element_type=F32)[:4]
    upper = jnp.dot(a, up_v[...], preferred_element_type=F32)[:4]
    r7[pas] = jnp.concatenate(
        [pack16(jnp.concatenate([gated, upper], axis=1)), split_sum(ss)], axis=1
    ).astype(BF)
    spread(r7, pas, pas_peers, 7)
    collect(r7, 16, 7)
    total = r7[0].astype(F32)
    for i in range(1, 16):
        total = total + r7[i].astype(F32)
    scale = rms(total[0:4, 640:641] + total[4:8, 640:641])
    scale = jnp.concatenate([scale, scale], axis=0)
    gated = total[0:8, :640] * scale
    upper = total[8:16, :640] * scale
    gelu = 0.5 * gated * (1.0 + jnp.tanh(0.7978845608028654 * (gated + 0.044715 * gated * gated * gated)))
    hidden = (gelu * upper).astype(BF)
    local[12].wait()
    low = jnp.dot(hidden, down_v[0:640], preferred_element_type=F32)
    high = jnp.dot(hidden, down_v[640:1280], preferred_element_type=F32)
    r8[tp] = pack8(low[:4] + high[4:8])
    spread(r8, tp, tp_peers, 8)
    collect(r8, 8, 8)
    whole = state2 + unpack8(jnp.sum(r8[...], axis=0))
    own = whole[:, 0:32]
    for t in range(1, 8):
        own = jnp.where(tp == t, whole[:, 32 * t : 32 * t + 32], own)
    out[...] = own

    for n, buf, count in (
        (0, r1a, 16),
        (1, r1b, 8),
        (2, r2, 4),
        (9, r2z, 4),
        (3, r3, 8),
        (4, r4, 4),
        (11, r4z, 4),
        (5, r5, 16),
        (6, r6, 8),
        (7, r7, 16),
        (8, r8, 8),
    ):
        wait_bytes(buf.at[pl.ds(0, count - 1)], es.at[n])
    wait_bytes(a_all.at[:, pl.ds(0, 7 * COLS)], big_s.at[0])
    wait_bytes(w_all.at[0, pl.ds(0, 12 * OWN)], big_s.at[1])
    wait_bytes(w_all.at[0, pl.ds(0, OWN)], big_s.at[3])

    @pl.when((zl > 0) & (zl < 3))
    def _():
        wait_bytes(w_all.at[0, pl.ds(0, 4 * OWN)], big_s.at[3])

    wait_bytes(w_all.at[0, pl.ds(0, 15 * OWN)], big_s.at[2])
    for c in outs:
        c.wait()


def finish(out_a, k_a, v_a, out_b, k_b, v_b):
    out_b[...] = out_a[...]
    k_b[...] = k_a[...]
    v_b[...] = v_a[...]


def shards(
    token_ids,
    embedding,
    passages,
    passage_lengths,
    w_key,
    w_value,
    norm_self,
    w_self_query,
    w_self_key,
    w_self_value,
    w_self_out,
    norm_cross,
    w_cross_query,
    w_cross_out,
    norm_ffn,
    w_gate,
    w_up,
    w_down,
):
    smem = pl.BlockSpec(memory_space=pltpu.SMEM)
    vmem = pl.BlockSpec(memory_space=pltpu.VMEM)
    hbm = pl.BlockSpec(memory_space=pltpu.HBM)
    dma = pltpu.SemaphoreType.DMA
    results = pl.pallas_call(
        kernel,
        name="decoder_layer",
        out_shape=(
            jax.ShapeDtypeStruct((STEPS, 32), F32),
            jax.ShapeDtypeStruct((ROWS, COLS), BF),
            jax.ShapeDtypeStruct((ROWS, COLS), BF),
        ),
        in_specs=[smem, smem, vmem, vmem, vmem] + [hbm] * 13,
        out_specs=(vmem, hbm, hbm),
        scratch_shapes=[
            pltpu.VMEM((ROWS, D), BF),
            pltpu.VMEM((2, D, COLS), BF),
            pltpu.VMEM((2, ROWS, COLS), BF),
            pltpu.VMEM((2, ROWS, COLS), F32),
            pltpu.VMEM((VROWS, D), BF),
            pltpu.VMEM((OWN, COLS), BF),
            pltpu.VMEM((OWN, COLS), BF),
            pltpu.VMEM((OWN, COLS), BF),
            pltpu.VMEM((COLS, OWN), BF),
            pltpu.VMEM((OWN, COLS), BF),
            pltpu.VMEM((COLS, OWN), BF),
            pltpu.VMEM((OWN, FFC), BF),
            pltpu.VMEM((OWN, FFC), BF),
            pltpu.VMEM((FFC, OWN), BF),
            pltpu.VMEM((16, 8, 128), F32),
            pltpu.VMEM((16, 8, 128), F32),
            pltpu.VMEM((8, 8, 128), F32),
            pltpu.VMEM((4, 8, 896), F32),
            pltpu.VMEM((4, 8, 896), F32),
            pltpu.VMEM((8, 8, 128), F32),
            pltpu.VMEM((4, 8, 384), F32),
            pltpu.VMEM((4, 8, 384), F32),
            pltpu.VMEM((16, 8, 384), F32),
            pltpu.VMEM((8, 8, 128), F32),
            pltpu.VMEM((16, 16, 768), BF),
            pltpu.VMEM((8, 8, 128), F32),
            dma((13,)),
            dma((2,)),
            dma((ACH,)),
            dma((2, ACH)),
            dma((2, ACH)),
            dma((6, WCH)),
            dma((3, 7, WCH)),
            dma((1,)),
            dma((4,)),
            dma((12,)),
            dma((12,)),
        ],
        compiler_params=pltpu.CompilerParams(
            collective_id=1, has_side_effects=True, vmem_limit_bytes=56 << 20
        ),
        cost_estimate=pl.CostEstimate(
            flops=2 * 2 * ROWS * COLS * D, bytes_accessed=16 << 20, transcendentals=1 << 20
        ),
    )(
        token_ids,
        passage_lengths,
        norm_self.reshape(32, 128),
        norm_cross.reshape(32, 128),
        norm_ffn.reshape(32, 128),
        passages,
        w_key,
        w_value,
        w_self_query,
        w_self_key,
        w_self_value,
        w_self_out,
        w_cross_query,
        w_cross_out,
        w_gate,
        w_up,
        w_down,
        embedding,
    )
    return pl.pallas_call(
        finish,
        name="finish",
        out_shape=tuple(jax.ShapeDtypeStruct(r.shape, r.dtype) for r in results),
        in_specs=[vmem] * 3,
        out_specs=(vmem, vmem, vmem),
        compiler_params=pltpu.CompilerParams(vmem_limit_bytes=56 << 20),
    )(*results)


def solution(mesh):
    in_specs = (
        P("pb"),
        P(("pas", "tp"), None),
        P(("pb", "pas"), "tp"),
        P(("pb", "pas")),
        P("pas", "tp"),
        P("pas", "tp"),
        P(),
        P("pas", "tp"),
        P("pas", "tp"),
        P("pas", "tp"),
        P("tp", "pas"),
        P(),
        P("pas", "tp"),
        P("tp", "pas"),
        P(),
        P("pas", "tp"),
        P("pas", "tp"),
        P("tp", "pas"),
    )
    out_specs = (P("pb", ("pas", "tp")), P(("pb", "pas"), "tp"), P(("pb", "pas"), "tp"))
    return jax.shard_map(shards, mesh=mesh, in_specs=in_specs, out_specs=out_specs, check_vma=False)
```

```python
import jax
import jax.numpy as jnp
from jax import lax
from jax.experimental import pallas as pl
from jax.experimental.pallas import tpu as pltpu
from jax.sharding import PartitionSpec as P

BF = jnp.bfloat16
F32 = jnp.float32
MESH = pl.DeviceIdType.MESH
D = 4096
DH = 64
PLEN = 256
STEPS = 4
ROWS = 512
COLS = 512
OWN = 256
FFC = 1280
VROWS = 251
AROW = (0, 128, 256, 384, 512)
ACH = len(AROW) - 1
STRAIGHT = ((1, 0), (1, 1), (1, 2), (1, 3))
WCH = 2
WRO = OWN // WCH
PASSED = tuple((1 if c % 2 == 0 else 3, c) for c in range(WCH))
KEPT = tuple((3 if c % 2 == 0 else 1, c) for c in range(WCH)) + tuple((2, c) for c in range(WCH))
HALF = D // 2

SCHEDULE = (
    ("sw",), ("sz", 0), ("sy", 0), ("sy", 1), ("sy", 2), ("sy", 3), ("e1",), ("wp", 0), ("wz", 1), ("wz", 4),
    ("sz", 1), ("ay", 0, 0), ("ay", 0, 1), ("c1",), ("wp", 1), ("wp", 4), ("wz", 2), ("wz", 5), ("az", 0),
    ("sz", 2), ("ay", 0, 2), ("ay", 0, 3), ("wk", 0), ("c2",), ("wp", 2), ("wp", 5), ("c2z",), ("wz", 3),
    ("wz", 6), ("az", 1), ("sz", 3), ("ay", 1, 0), ("wp", 6), ("wk", 1), ("wk", 4), ("ay", 1, 1), ("wp", 3),
    ("c3",), ("az", 2), ("wk", 2), ("wk", 5), ("ay", 1, 2), ("c4",), ("az", 3), ("wk", 3), ("wk", 6),
    ("c4z",), ("mm",), ("ay", 1, 3), ("mm", 0), ("c5",), ("mm", 1),
)


def pack8(v):
    n = v.shape[1] // 2
    return jnp.concatenate([v[:, :n], v[:, n:]], axis=0)


def unpack8(p):
    return jnp.concatenate([p[:4], p[4:8]], axis=1)


def pack16(v):
    n = v.shape[1] // 4
    return jnp.concatenate([v[:, n * k : n * k + n] for k in range(4)], axis=0)


def unpack16(p):
    return jnp.concatenate([p[4 * k : 4 * k + 4] for k in range(4)], axis=1)


def pad8(v):
    return jnp.concatenate([v, jnp.zeros_like(v)], axis=0)


def head_mask():
    head = lax.broadcasted_iota(jnp.int32, (8, COLS), 0)
    lane = lax.broadcasted_iota(jnp.int32, (8, COLS), 1)
    return jnp.where((lane >= head * DH) & (lane < head * DH + DH), 1.0, 0.0).astype(F32)


def by_head(q):
    mask = head_mask()
    return jnp.concatenate([q[s : s + 1] * mask for s in range(STEPS)], axis=0).astype(BF)


def own_head(acc):
    mask = head_mask()
    rows = [
        jnp.sum(acc[8 * s : 8 * s + 8] * mask, axis=0, keepdims=True) for s in range(STEPS)
    ]
    return jnp.concatenate(rows, axis=0)


def attend(q, keys, values, live):
    scores = lax.dot_general(
        by_head(q), keys, (((1,), (1,)), ((), ())), preferred_element_type=F32
    ) * (1.0 / DH**0.5)
    scores = jnp.where(live, scores, -1e30)
    peak = jnp.max(scores, axis=1, keepdims=True)
    weights = jnp.where(live, jnp.exp(scores - peak), 0.0).astype(BF)
    total = jnp.sum(weights.astype(F32), axis=1, keepdims=True)
    accum = jnp.dot(weights, values, preferred_element_type=F32)
    return peak, total, accum


def halve(total):
    parts = [
        jnp.concatenate([total[:, 256 * n : 256 * n + 128], total[:, 256 * n + 128 : 256 * n + 256]], axis=0)
        for n in range(3)
    ]
    ss = total[:, 768:896]
    hi = ss.astype(BF).astype(F32)
    parts.append(jnp.concatenate([hi, ss - hi], axis=0))
    return jnp.concatenate(parts, axis=1).astype(BF)


def split_sum(ss):
    hi = ss.astype(BF).astype(F32)
    lo = ss - hi
    z = jnp.zeros_like(ss)
    return jnp.broadcast_to(jnp.concatenate([hi, lo, z, z], axis=0), (16, 128))


def kernel(
    tok,
    lens,
    g_self,
    g_cross,
    g_ffn,
    passages,
    w_key,
    w_value,
    w_sq,
    w_sk,
    w_sv,
    w_so,
    w_cq,
    w_co,
    w_gate,
    w_up,
    w_down,
    emb,
    out,
    kout,
    vout,
    a_all,
    w_all,
    kv,
    sums,
    emb_v,
    sq_v,
    sk_v,
    sv_v,
    so_v,
    cq_v,
    co_v,
    gate_v,
    up_v,
    down_v,
    s1a,
    r1a,
    r1b,
    r2,
    r2z,
    r3,
    r4,
    r4z,
    r5,
    r6,
    r7,
    r8,
    lsem,
    osem,
    az_r,
    af_r,
    an_r,
    wz_r,
    wx_r,
    ws_r,
    big_s,
    es,
    er,
):
    pb = lax.axis_index("pb")
    pas = lax.axis_index("pas")
    tp = lax.axis_index("tp")
    x, zl = pas // 4, pas % 4
    zh, y = tp // 4, tp % 4
    xs = [(x + k) % 4 for k in range(4)]
    zs = [(zl + k) % 4 for k in range(4)]
    ys = [(y + k) % 4 for k in range(4)]
    xb = [(x - k + 4) % 4 for k in range(4)]
    zb = [(zl - k + 4) % 4 for k in range(4)]
    yb = [(y - k + 4) % 4 for k in range(4)]
    far = (2, 1, 3, 0)
    pas_peers = [
        (pb, xs[a] * 4 + zs[b], tp) for a in far for b in (3, 2, 1, 0) if (a, b) != (0, 0)
    ]
    tp_peers = [
        (pb, pas, (zh * 4 if b == 0 else (1 - zh) * 4) + ys[a])
        for b in (1, 0)
        for a in far
        if (a, b) != (0, 0)
    ]
    x_peers = {k: (pb, xs[k] * 4 + zl, tp) for k in (1, 3, 2)}
    z_peers = {k: (pb, x * 4 + zs[k], tp) for k in (1, 3, 2)}
    y_peers = {k: (pb, pas, zh * 4 + ys[k]) for k in (1, 3, 2)}
    z4_peer = (pb, pas, (1 - zh) * 4 + y)
    sibling = (1 - pb, pas, tp)

    barrier = pltpu.get_barrier_semaphore()
    greet = pas_peers + tp_peers + [sibling]
    for d in greet:
        pl.semaphore_signal(barrier, inc=1, device_id=d, device_id_type=MESH)

    pas0 = pl.multiple_of(pas * OWN, OWN)
    tp0 = pl.multiple_of(tp * COLS, COLS)
    loads = [
        (passages, a_all.at[:, pl.ds(tp0, COLS)]),
        (w_key, w_all.at[0, pl.ds(pas0, OWN)]),
        (w_value, w_all.at[1, pl.ds(pas0, OWN)]),
        (emb, emb_v),
        (w_sq, sq_v),
        (w_sk, sk_v),
        (w_sv, sv_v),
        (w_so, so_v),
        (w_cq, cq_v),
        (w_co, co_v),
        (w_gate, gate_v),
        (w_up, up_v),
        (w_down, down_v),
    ]
    local = [pltpu.make_async_copy(s, d, lsem.at[n]) for n, (s, d) in enumerate(loads)]
    for c in local[:3]:
        c.start()

    def send(src, dst, ssem, rsem, dev):
        pltpu.make_async_remote_copy(
            src_ref=src,
            dst_ref=dst,
            send_sem=ssem,
            recv_sem=rsem,
            device_id=dev,
            device_id_type=MESH,
        ).start()

    def wait_bytes(ref, sem):
        pltpu.make_async_copy(ref, ref, sem).wait()

    def a_piece(block, c):
        cols = pl.ds(pl.multiple_of(block * COLS, COLS), COLS)
        return a_all.at[pl.ds(AROW[c], AROW[c + 1] - AROW[c]), cols]

    def w_piece(block, c):
        return w_all.at[pb, pl.ds(pl.multiple_of(block * OWN + c * WRO, WRO), WRO)]

    def a_to_z(c):
        piece = a_piece(tp, c)
        send(piece, piece, big_s.at[0], az_r.at[c], z4_peer)

    def a_to_y(half, block, c):
        piece = a_piece(block, c)
        for k, passed_on in ((1, c % 2 == 0), (3, c % 2 == 1)):
            passed_on = passed_on and (half, c) not in STRAIGHT
            rsem = af_r.at[half, c] if passed_on else an_r.at[half, c]
            send(piece, piece, big_s.at[0], rsem, y_peers[k])
        if (half, c) in STRAIGHT:
            send(piece, piece, big_s.at[0], an_r.at[half, c], y_peers[2])

    def a_from_z(c):
        block = (1 - zh) * 4 + y
        wait_bytes(a_piece(block, c), az_r.at[c])
        a_to_y(1, block, c)

    def a_from_y(half, c):
        if (half, c) in STRAIGHT:
            return
        k = 1 if c % 2 == 0 else 3
        block = (zh if half == 0 else 1 - zh) * 4 + yb[k]
        piece = a_piece(block, c)
        wait_bytes(piece, af_r.at[half, c])
        send(piece, piece, big_s.at[0], an_r.at[half, c], y_peers[k])

    def w_sibling(block, c):
        piece = w_piece(block, c)
        send(piece, piece, big_s.at[2], ws_r.at[0], sibling)

    def w_to_x(block, e, c):
        piece = w_piece(block, c)
        for k in (1, 3):
            send(piece, piece, big_s.at[1], wx_r.at[k - 1, e, c], x_peers[k])

    def w_to_z(block, up, n, c):
        piece = w_piece(block, c)

        @pl.when(zl < 3 if up else zl > 0)
        def _():
            to = (pb, pas + 1, tp) if up else (pb, pas - 1, tp)
            send(piece, piece, big_s.at[3], wz_r.at[n if up else n + 3, c], to)

    def origin(e):
        if e == 0:
            return None, zl
        if e < 4:
            return zl >= e, zl - e
        return zl + (e - 3) < 4, zl + (e - 3)

    def guarded(e, body):
        here, bz = origin(e)
        if here is None:
            body(bz)
        else:
            pl.when(here)(lambda: body(bz))

    def w_from_z(e):
        def body(bz):
            block = x * 4 + bz
            for c in range(WCH):
                wait_bytes(w_piece(block, c), wz_r.at[e - 1, c])
                if e not in (3, 6):
                    w_to_z(block, e < 4, e if e < 4 else e - 3, c)
                w_to_x(block, e, c)
                w_sibling(block, c)

        guarded(e, body)

    def w_from_x(e, pieces):
        def body(bz):
            for kx, c in pieces:
                block = xb[kx] * 4 + bz
                piece = w_piece(block, c)
                wait_bytes(piece, wx_r.at[kx - 1, e, c])
                if (kx, c) in PASSED:
                    send(piece, piece, big_s.at[1], wx_r.at[1, e, c], x_peers[kx])
                w_sibling(block, c)

        guarded(e, body)

    def spread(buf, me, peers, n):
        slot = buf.at[me]
        for p in peers:
            send(slot, slot, es.at[n], er.at[n], p)

    def collect(buf, count, n):
        wait_bytes(buf.at[pl.ds(0, count - 1)], er.at[n])

    def merge_pas(part, bx, bz, n):
        bx[x] = part
        for k in (2, 1, 3):
            send(bx.at[x], bx.at[x], es.at[n], er.at[n], x_peers[k])

    def merge_pas_z(bx, bz, n):
        wait_bytes(bx.at[pl.ds(0, 3)], er.at[n])
        total = bx[0] + bx[1] + bx[2] + bx[3]
        bz[zl] = total if bz.dtype == F32 else halve(total)
        for k in (3, 2, 1):
            send(bz.at[zl], bz.at[zl], es.at[n + 7], er.at[n + 7], z_peers[k])

    def merged(bz, n):
        wait_bytes(bz.at[pl.ds(0, 3)], er.at[n + 7])
        return bz[0] + bz[1] + bz[2] + bz[3]

    def gain(g):
        return jnp.concatenate([g[pl.ds(2 * pas, 1), :], g[pl.ds(2 * pas + 1, 1), :]], axis=1)

    pl.semaphore_wait(barrier, len(greet))
    for n in range(3):
        local[n].wait()
    for c in local[3:]:
        c.start()
    st = {}

    def e1():
        local[3].wait()
        row = lax.broadcasted_iota(jnp.int32, (8, VROWS), 0)
        place = lax.broadcasted_iota(jnp.int32, (8, VROWS), 1) + (pas * 8 + tp) * VROWS
        wanted = jnp.full((8, VROWS), -1, jnp.int32)
        for s in range(STEPS):
            wanted = jnp.where(row == s, tok[s], wanted)
        onehot = jnp.where(place == wanted, 1.0, 0.0).astype(BF)
        mine = jnp.dot(onehot, emb_v[...], preferred_element_type=F32)
        for i in range(16):
            s1a[i] = pack8(mine[:4, OWN * i : OWN * i + OWN])
        r1a[pas] = s1a[pas]
        for p in pas_peers:
            send(s1a.at[p[1]], r1a.at[pas], es.at[0], er.at[0], p)

    def c1():
        collect(r1a, 16, 0)
        r1b[tp] = jnp.sum(r1a[...], axis=0)
        spread(r1b, tp, tp_peers, 1)

    def scaled(state, g):
        ss = jnp.sum(state * state, axis=1, keepdims=True)
        return pad8(state * gain(g)).astype(BF), ss

    def rms(ss):
        return lax.rsqrt(ss * (1.0 / D) + 1e-06)

    def c2():
        collect(r1b, 8, 1)
        st["state0"] = unpack8(jnp.sum(r1b[...], axis=0))
        a, ss = scaled(st["state0"], g_self)
        parts = []
        for n, w in ((4, sq_v), (5, sk_v), (6, sv_v)):
            local[n].wait()
            parts.append(pack8(jnp.dot(a, w[...], preferred_element_type=F32)[:4]))
        parts.append(jnp.broadcast_to(pad8(ss), (8, 128)))
        merge_pas(jnp.concatenate(parts, axis=1), r2, r2z, 2)

    def c2z():
        merge_pas_z(r2, r2z, 2)

    def c3():
        wait_bytes(r2z.at[pl.ds(0, 3)], er.at[9])
        total = r2z[0].astype(F32)
        for i in range(1, 4):
            total = total + r2z[i].astype(F32)
        scale = rms(total[:4, 384:385] + total[8:12, 384:385])
        whole = [
            jnp.concatenate([total[:8, 128 * n : 128 * n + 128], total[8:, 128 * n : 128 * n + 128]], axis=1)
            for n in range(3)
        ]
        q, k, v = [unpack8(w) * scale for w in whole]
        none = jnp.zeros((124, COLS), F32)
        keys = jnp.concatenate([k, none], axis=0).astype(BF)
        values = jnp.concatenate([v, none], axis=0).astype(BF)
        step = lax.broadcasted_iota(jnp.int32, (32, 128), 0)
        other = lax.broadcasted_iota(jnp.int32, (32, 128), 1)
        _, weight, accum = attend(q.astype(BF).astype(F32), keys, values, other * 8 <= step)
        heads = own_head(accum / weight)
        local[7].wait()
        r3[tp] = pack8(jnp.dot(pad8(heads).astype(BF), so_v[...], preferred_element_type=F32)[:4])
        spread(r3, tp, tp_peers, 3)

    def c4():
        collect(r3, 8, 3)
        st["state1"] = st["state0"] + unpack8(jnp.sum(r3[...], axis=0))
        a, ss = scaled(st["state1"], g_cross)
        local[8].wait()
        part = jnp.dot(a, cq_v[...], preferred_element_type=F32)[:4]
        part = jnp.concatenate([pack8(part), jnp.broadcast_to(pad8(ss), (8, 128))], axis=1)
        merge_pas(part, r4, r4z, 4)

    def c4z():
        merge_pas_z(r4, r4z, 4)

    def c5():
        total = merged(r4z, 4)
        st["cquery"] = unpack8(total[:, :256]) * rms(total[:4, 256:257])

    near = pl.ds(pl.multiple_of(zh * HALF, HALF), HALF)
    distant = pl.ds(pl.multiple_of((1 - zh) * HALF, HALF), HALF)

    def a_whole(half, c):
        blocks = 3 if (half, c) in STRAIGHT else 2
        n = AROW[c + 1] - AROW[c]
        wait_bytes(a_all.at[pl.ds(0, n), pl.ds(0, blocks * COLS)], an_r.at[half, c])

    def mm(part=None):
        if part is None:
            for c in range(ACH):
                a_whole(0, c)
            wait_bytes(w_all.at[0, pl.ds(0, 15 * OWN)], ws_r.at[0])
            rows, cols = pl.ds(0, ROWS), near
        else:
            for c in (2 * part, 2 * part + 1):
                a_whole(1, c)
            first, last = AROW[2 * part], AROW[2 * part + 2]
            rows, cols = pl.ds(first, last - first), distant
        for c in range(2):

            def tile(n, carry):
                to = pl.ds(pl.multiple_of(n * 256, 256), 256)
                new = jnp.dot(a_all[rows, cols], w_all[c, cols, to], preferred_element_type=F32)
                if part is None:
                    sums[c, rows, to] = new
                else:
                    kv[c, rows, to] = (sums[c, rows, to] + new).astype(BF)
                return carry

            lax.fori_loop(0, 2, tile, 0)

    def sw():
        for c in range(WCH):
            w_to_z(pas, True, 0, c)
            w_to_z(pas, False, 0, c)
            w_to_x(pas, 0, c)

    def sy(c):
        a_to_y(0, tp, c)

    events = {
        "sz": a_to_z,
        "sw": sw,
        "sy": sy,
        "az": a_from_z,
        "ay": a_from_y,
        "wz": w_from_z,
        "wp": lambda e: w_from_x(e, PASSED),
        "wk": lambda e: w_from_x(e, KEPT),
        "e1": e1,
        "c1": c1,
        "c2": c2,
        "c2z": c2z,
        "c3": c3,
        "c4": c4,
        "c4z": c4z,
        "c5": c5,
        "mm": mm,
    }
    for event in SCHEDULE:
        events[event[0]](*event[1:])
    state1, cquery = st["state1"], st["cquery"]
    outs = [
        pltpu.make_async_copy(kv.at[0], kout, osem.at[0]),
        pltpu.make_async_copy(kv.at[1], vout, osem.at[1]),
    ]
    for c in outs:
        c.start()

    slot = lax.broadcasted_iota(jnp.int32, (32, ROWS), 1)
    live = (slot < lens[0]) | ((slot >= PLEN) & (slot < lens[1] + PLEN))
    peak, weight, accum = attend(cquery.astype(BF).astype(F32), kv[0], kv[1], live)
    head = lax.broadcasted_iota(jnp.int32, (8, 128), 0)
    lane = lax.broadcasted_iota(jnp.int32, (8, 128), 1)
    rows = []
    for g in range(2):
        for s in range(STEPS):
            both = jnp.where(lane == head - 4 * g, peak[8 * s : 8 * s + 8], 0.0) + jnp.where(
                (lane >= 64) & (lane - 64 == head - 4 * g), weight[8 * s : 8 * s + 8], 0.0
            )
            rows.append(jnp.sum(both, axis=0, keepdims=True))
    r5[pas] = jnp.concatenate([pack8(own_head(accum)), jnp.concatenate(rows, axis=0)], axis=1)
    spread(r5, pas, pas_peers, 5)
    collect(r5, 16, 5)
    peaks = [r5[i, :, 256:384] for i in range(16)]
    top = peaks[0]
    for i in range(1, 16):
        top = jnp.maximum(top, peaks[i])
    shares = []
    weight = jnp.zeros((8, 128), F32)
    for i in range(16):
        share = jnp.where(lane < 4, jnp.exp(peaks[i] - top), 0.0)
        weight = weight + share * pltpu.roll(peaks[i], 64, 1)
        shares.append(share)
    inv = 1.0 / jnp.where(lane < 4, weight, 1.0)
    shares = jnp.concatenate([s * inv for s in shares], axis=0)
    lane_of = lax.broadcasted_iota(jnp.int32, (128, 256), 0)
    column = lax.broadcasted_iota(jnp.int32, (128, 256), 1)
    widen = jnp.where((column >= lane_of * DH) & (column < lane_of * DH + DH), 1.0, 0.0)
    wide = jnp.dot(
        shares, widen.astype(F32), preferred_element_type=F32, precision=lax.Precision.HIGHEST
    )
    mixed = jnp.zeros((8, 256), F32)
    for i in range(16):
        mixed = mixed + wide[8 * i : 8 * i + 8] * r5[i, :, :256]
    local[9].wait()
    heads = pad8(unpack8(mixed)).astype(BF)
    r6[tp] = pack8(jnp.dot(heads, co_v[...], preferred_element_type=F32)[:4])
    spread(r6, tp, tp_peers, 6)
    collect(r6, 8, 6)
    state2 = state1 + unpack8(jnp.sum(r6[...], axis=0))

    a, ss = scaled(state2, g_ffn)
    local[10].wait()
    local[11].wait()
    gated = jnp.dot(a, gate_v[...], preferred_element_type=F32)[:4]
    upper = jnp.dot(a, up_v[...], preferred_element_type=F32)[:4]
    r7[pas] = jnp.concatenate(
        [pack16(jnp.concatenate([gated, upper], axis=1)), split_sum(ss)], axis=1
    ).astype(BF)
    spread(r7, pas, pas_peers, 7)
    collect(r7, 16, 7)
    total = r7[0].astype(F32)
    for i in range(1, 16):
        total = total + r7[i].astype(F32)
    scale = rms(total[0:4, 640:641] + total[4:8, 640:641])
    scale = jnp.concatenate([scale, scale], axis=0)
    gated = total[0:8, :640] * scale
    upper = total[8:16, :640] * scale
    gelu = 0.5 * gated * (1.0 + jnp.tanh(0.7978845608028654 * (gated + 0.044715 * gated * gated * gated)))
    hidden = (gelu * upper).astype(BF)
    local[12].wait()
    low = jnp.dot(hidden, down_v[0:640], preferred_element_type=F32)
    high = jnp.dot(hidden, down_v[640:1280], preferred_element_type=F32)
    r8[tp] = pack8(low[:4] + high[4:8])
    spread(r8, tp, tp_peers, 8)
    collect(r8, 8, 8)
    whole = state2 + unpack8(jnp.sum(r8[...], axis=0))
    own = whole[:, 0:32]
    for t in range(1, 8):
        own = jnp.where(tp == t, whole[:, 32 * t : 32 * t + 32], own)
    out[...] = own

    for n, buf, count in (
        (0, r1a, 16),
        (1, r1b, 8),
        (2, r2, 4),
        (9, r2z, 4),
        (3, r3, 8),
        (4, r4, 4),
        (11, r4z, 4),
        (5, r5, 16),
        (6, r6, 8),
        (7, r7, 16),
        (8, r8, 8),
    ):
        wait_bytes(buf.at[pl.ds(0, count - 1)], es.at[n])
    wait_bytes(a_all.at[:, pl.ds(0, 7 * COLS)], big_s.at[0])
    wait_bytes(w_all.at[0, pl.ds(0, 12 * OWN)], big_s.at[1])
    wait_bytes(w_all.at[0, pl.ds(0, OWN)], big_s.at[3])

    @pl.when((zl > 0) & (zl < 3))
    def _():
        wait_bytes(w_all.at[0, pl.ds(0, 4 * OWN)], big_s.at[3])

    wait_bytes(w_all.at[0, pl.ds(0, 15 * OWN)], big_s.at[2])
    for c in outs:
        c.wait()


def finish(out_a, k_a, v_a, out_b, k_b, v_b):
    out_b[...] = out_a[...]
    k_b[...] = k_a[...]
    v_b[...] = v_a[...]


def shards(
    token_ids,
    embedding,
    passages,
    passage_lengths,
    w_key,
    w_value,
    norm_self,
    w_self_query,
    w_self_key,
    w_self_value,
    w_self_out,
    norm_cross,
    w_cross_query,
    w_cross_out,
    norm_ffn,
    w_gate,
    w_up,
    w_down,
):
    smem = pl.BlockSpec(memory_space=pltpu.SMEM)
    vmem = pl.BlockSpec(memory_space=pltpu.VMEM)
    hbm = pl.BlockSpec(memory_space=pltpu.HBM)
    dma = pltpu.SemaphoreType.DMA
    results = pl.pallas_call(
        kernel,
        name="decoder_layer",
        out_shape=(
            jax.ShapeDtypeStruct((STEPS, 32), F32),
            jax.ShapeDtypeStruct((ROWS, COLS), BF),
            jax.ShapeDtypeStruct((ROWS, COLS), BF),
        ),
        in_specs=[smem, smem, vmem, vmem, vmem] + [hbm] * 13,
        out_specs=(vmem, hbm, hbm),
        scratch_shapes=[
            pltpu.VMEM((ROWS, D), BF),
            pltpu.VMEM((2, D, COLS), BF),
            pltpu.VMEM((2, ROWS, COLS), BF),
            pltpu.VMEM((2, ROWS, COLS), F32),
            pltpu.VMEM((VROWS, D), BF),
            pltpu.VMEM((OWN, COLS), BF),
            pltpu.VMEM((OWN, COLS), BF),
            pltpu.VMEM((OWN, COLS), BF),
            pltpu.VMEM((COLS, OWN), BF),
            pltpu.VMEM((OWN, COLS), BF),
            pltpu.VMEM((COLS, OWN), BF),
            pltpu.VMEM((OWN, FFC), BF),
            pltpu.VMEM((OWN, FFC), BF),
            pltpu.VMEM((FFC, OWN), BF),
            pltpu.VMEM((16, 8, 128), F32),
            pltpu.VMEM((16, 8, 128), F32),
            pltpu.VMEM((8, 8, 128), F32),
            pltpu.VMEM((4, 8, 896), F32),
            pltpu.VMEM((4, 16, 512), BF),
            pltpu.VMEM((8, 8, 128), F32),
            pltpu.VMEM((4, 8, 384), F32),
            pltpu.VMEM((4, 8, 384), F32),
            pltpu.VMEM((16, 8, 384), F32),
            pltpu.VMEM((8, 8, 128), F32),
            pltpu.VMEM((16, 16, 768), BF),
            pltpu.VMEM((8, 8, 128), F32),
            dma((13,)),
            dma((2,)),
            dma((ACH,)),
            dma((2, ACH)),
            dma((2, ACH)),
            dma((6, WCH)),
            dma((3, 7, WCH)),
            dma((1,)),
            dma((4,)),
            dma((12,)),
            dma((12,)),
        ],
        compiler_params=pltpu.CompilerParams(
            collective_id=1, has_side_effects=True, vmem_limit_bytes=56 << 20
        ),
        cost_estimate=pl.CostEstimate(
            flops=2 * 2 * ROWS * COLS * D, bytes_accessed=16 << 20, transcendentals=1 << 20
        ),
    )(
        token_ids,
        passage_lengths,
        norm_self.reshape(32, 128),
        norm_cross.reshape(32, 128),
        norm_ffn.reshape(32, 128),
        passages,
        w_key,
        w_value,
        w_self_query,
        w_self_key,
        w_self_value,
        w_self_out,
        w_cross_query,
        w_cross_out,
        w_gate,
        w_up,
        w_down,
        embedding,
    )
    return pl.pallas_call(
        finish,
        name="finish",
        out_shape=tuple(jax.ShapeDtypeStruct(r.shape, r.dtype) for r in results),
        in_specs=[vmem] * 3,
        out_specs=(vmem, vmem, vmem),
        compiler_params=pltpu.CompilerParams(vmem_limit_bytes=56 << 20),
    )(*results)


def solution(mesh):
    in_specs = (
        P("pb"),
        P(("pas", "tp"), None),
        P(("pb", "pas"), "tp"),
        P(("pb", "pas")),
        P("pas", "tp"),
        P("pas", "tp"),
        P(),
        P("pas", "tp"),
        P("pas", "tp"),
        P("pas", "tp"),
        P("tp", "pas"),
        P(),
        P("pas", "tp"),
        P("tp", "pas"),
        P(),
        P("pas", "tp"),
        P("pas", "tp"),
        P("tp", "pas"),
    )
    out_specs = (P("pb", ("pas", "tp")), P(("pb", "pas"), "tp"), P(("pb", "pas"), "tp"))
    return jax.shard_map(shards, mesh=mesh, in_specs=in_specs, out_specs=out_specs, check_vma=False)
```
